32 devices in a mesh: doc: 4 (over y, x), ctx: 8 (over z, core).
Axes of the slice: x: 2, y: 2, z: 4, core: 2. Of those that a mesh axis runs over, the one named last changes fastest.
Arguments:
- queries: bfloat16 [4, 1024, 4096], P('doc', 'ctx'), may hold values from -6 to 6, as said below
- key_heads: bfloat16 [4, 1024, 512], P('doc', 'ctx'), may hold values from -6 to 6, as said below
- value_heads: bfloat16 [4, 1024, 512], P('doc', 'ctx'), may hold values from -6 to 6
- out_grad: bfloat16 [4, 1024, 4096], P('doc', 'ctx'), may hold values from -6 to 6
- log_sums: float32 [4, 32, 1024], P('doc', 'ctx'), as said below
- row_delta: float32 [4, 32, 1024], P('doc', 'ctx'), may hold values from -6 to 6
- doc_start: int32 [4], P('doc'), may hold values from 0 to 512, as said below
- layer_input: bfloat16 [4, 1024, 8192], P('doc', 'ctx'), may hold values from -6 to 6
- hash_in: int32 [8192], replicated, may hold values from 0 to 255
- hash_out: int32 [4096], P('ctx'), may hold values from 0 to 127
- query_sketch: bfloat16 [4096, 8192], P('doc', 'ctx'), may hold values from -6 to 6
Outputs:
- doc_sketch: float32 [4, 8192], P('doc', 'ctx')
- scores: float32 [4, 4096], P(None, ('doc', 'ctx'))
The draws below stay inside these ranges and needn't reach their ends.
Inputs may be any that keep to these rules, and one draw needn't show every extreme that they name: `queries`: drawn together with key_heads; float values. `key_heads`: drawn together with queries; float values. log_sums[e, h, i] is the log of the sum of exp(logits[i, j]) over the positions j visible to i, for the given queries and key_heads; 0 for rows before doc_start[e]. `doc_start`: some document starts at 0 and some at 512.
All inputs are finite; a program needn't handle non-finite values.
Results may differ from the reference program's by a relative error of at most 0.024.
Values may be sent and summed in bfloat16 or wider, within the bound.
No kernel may reach another device: no remote copies, remote signals or barrier semaphores. Data moves between devices by JAX's collectives and lax.ppermute only.
A program may use at most 128 MiB of HBM per device.

```python
import jax
import jax.numpy as jnp
from jax import lax

D = 8192
HD = 128
HEADS = 32
KVH = 4
K1 = 128
K2 = 64
QUERIES = 4096
DOCS = 4
SEQ = 1024
GROUP = 8
SK = 8192


def make_common(key):
    base = jax.random.fold_in(key, 11)
    key_query, key_key, key_start, key_order = jax.random.split(base, 4)
    query_float = jnp.clip(jax.random.normal(key_query, (DOCS, SEQ, HEADS * HD), jnp.float32), -6.0, 6.0)
    key_float = jnp.clip(jax.random.normal(key_key, (DOCS, SEQ, KVH * HD), jnp.float32), -6.0, 6.0)
    starts = jax.random.randint(key_start, (DOCS,), 0, SEQ // 2 + 1, dtype=jnp.int32)
    order = jax.random.permutation(key_order, DOCS)
    starts = starts.at[order[0]].set(0).at[order[1]].set(SEQ // 2)
    return (query_float.astype(jnp.bfloat16), key_float.astype(jnp.bfloat16), starts.astype(jnp.int32))


def draw_queries(key, part):
    return make_common(key)[0]


def draw_key_heads(key, part):
    return make_common(key)[1]


def draw_doc_start(key, part):
    return make_common(key)[2]


def draw_log_sums(key, part):
    query_all, key_all, starts = make_common(key)
    factor = HD ** (-0.5)
    places = jnp.arange(SEQ, dtype=jnp.int32)

    def one_item(item):
        doc_number = item // HEADS
        head_number = item % HEADS
        query_doc = lax.dynamic_index_in_dim(query_all, doc_number, 0, keepdims=False).reshape(SEQ, HEADS, HD)
        key_doc = lax.dynamic_index_in_dim(key_all, doc_number, 0, keepdims=False).reshape(SEQ, KVH, HD)
        query_head = lax.dynamic_index_in_dim(query_doc, head_number, 1, keepdims=False)
        key_head = lax.dynamic_index_in_dim(key_doc, head_number // GROUP, 1, keepdims=False)
        logits = jnp.dot(query_head, key_head.T, preferred_element_type=jnp.float32) * factor
        first_pos = lax.dynamic_index_in_dim(starts, doc_number, 0, keepdims=False)
        visible = (places[None, :] <= places[:, None]) & (places[None, :] >= first_pos)
        masked = jnp.where(visible, logits, -1e+30)
        top_value = jnp.max(masked, axis=1)
        has_keys = places >= first_pos
        safe_top = jnp.where(has_keys, top_value, 0.0)
        totals = jnp.sum(jnp.where(visible, jnp.exp(logits - safe_top[:, None]), 0.0), axis=1)
        safe_total = jnp.where(has_keys, totals, 1.0)
        return jnp.where(has_keys, safe_top + jnp.log(safe_total), 0.0)
    result = lax.map(one_item, jnp.arange(DOCS * HEADS, dtype=jnp.int32))
    return result.reshape(DOCS, HEADS, SEQ).astype(jnp.float32)


def set_ends(drawn, own_key, smallest, high):
    longest = drawn.shape.index(max(drawn.shape))
    spots = []
    for shift in (0, 1):
        where = [jax.random.randint(jax.random.fold_in(own_key, axis), (), 0, length) for axis, length in enumerate(drawn.shape)]
        where[longest] = (where[longest] + shift) % drawn.shape[longest]
        spots.append(tuple(where))
    return drawn.at[spots[0]].set(smallest).at[spots[1]].set(high)


def shard_levels(own_key, extent, shards, least, high):
    gain = 1.0
    for axis_at, shards_of in shards:
        steps = jax.random.uniform(jax.random.fold_in(jax.random.fold_in(own_key, 6), axis_at), (shards_of,), jnp.float32, least / len(shards), high / len(shards))
        gain = gain * jnp.repeat(jnp.exp(steps), extent[axis_at] // shards_of).reshape((-1,) + (1,) * (len(extent) - 1 - axis_at))
    return gain


def noise(key, dims, deviation, most, shards=(), held_as=jnp.bfloat16):
    loudness = shard_levels(key, dims, shards, -0.22, 0.18) if shards else 1.0
    array = jax.random.normal(key, dims, jnp.float32) * deviation * loudness
    return jnp.minimum(jnp.maximum(array, -most), most).astype(held_as)


def setup_inputs(seed: int = 0) -> dict:
    key_list = jax.random.split(jax.random.key(seed), 12)
    queries = draw_queries(jax.random.fold_in(key_list[11], 71), 0)
    key_heads = draw_key_heads(jax.random.fold_in(key_list[11], 71), 0)
    value_heads = noise(key_list[2], (DOCS, SEQ, KVH * HD), 1.0, 6.0, ((0, 4), (1, 8)))
    out_grad = noise(key_list[3], (DOCS, SEQ, HEADS * HD), 1.0, 6.0, ((0, 4), (1, 8)))
    log_sums = draw_log_sums(jax.random.fold_in(key_list[11], 71), 0)
    row_delta = noise(key_list[5], (DOCS, HEADS, SEQ), 1.0, 6.0, ((0, 4), (1, 8)), jnp.float32)
    doc_start = draw_doc_start(jax.random.fold_in(key_list[11], 71), 0)
    layer_input = noise(key_list[7], (DOCS, SEQ, D), 1.0, 6.0, ((0, 4), (1, 8)))
    hash_in = set_ends(jax.random.randint(key_list[8], (D,), 0, 2 * K1), jax.random.fold_in(key_list[8], 1), 0, (2 * K1) - 1).astype(jnp.int32)
    hash_out = set_ends(jax.random.randint(key_list[9], (HEADS * HD,), 0, 2 * K2), jax.random.fold_in(key_list[9], 1), 0, (2 * K2) - 1).astype(jnp.int32)
    query_sketch = noise(key_list[10], (QUERIES, SK), 1.0, 6.0, ((0, 4), (1, 8)))
    return {"queries": queries, "key_heads": key_heads, "value_heads": value_heads, "out_grad": out_grad, "log_sums": log_sums, "row_delta": row_delta, "doc_start": doc_start, "layer_input": layer_input, "hash_in": hash_in, "hash_out": hash_out, "query_sketch": query_sketch}


def sign_table(codes, buckets):
    levels = jnp.arange(buckets, dtype=jnp.int32)
    plus_part = (codes[..., None] == levels).astype(jnp.float32)
    minus_part = (codes[..., None] == levels + buckets).astype(jnp.float32)
    return plus_part - minus_part


def attend_head(query_head, key_head, value_head, grad_head, log_head, delta_head, first_pos):
    factor = HD ** -0.5
    logits = jnp.dot(query_head, key_head.T, preferred_element_type=jnp.float32) * factor
    places = jnp.arange(SEQ, dtype=jnp.int32)
    visible = (places[None, :] <= places[:, None]) & (places[None, :] >= first_pos)
    weights = jnp.where(visible, jnp.exp(logits - log_head[:, None]), 0.0)
    grad_weights = jnp.dot(grad_head, value_head.T, preferred_element_type=jnp.float32)
    grad_scores = (weights * (grad_weights - delta_head[:, None])).astype(jnp.bfloat16)
    product = jnp.dot(grad_scores, key_head, preferred_element_type=jnp.float32)
    return (product * factor).astype(jnp.bfloat16)


def reference(queries, key_heads, value_heads, out_grad, log_sums, row_delta, doc_start, layer_input, hash_in, hash_out, query_sketch):
    table_in = sign_table(hash_in, K1)
    table_out = sign_table(hash_out.reshape(HEADS, HD), K2)

    def one_document(items):
        query_doc, key_doc, value_doc, grad_doc, log_doc, delta_doc, first_pos, input_doc = items
        query_three = query_doc.reshape(SEQ, HEADS, HD)
        grad_three = grad_doc.reshape(SEQ, HEADS, HD)
        key_three = key_doc.reshape(SEQ, KVH, HD)
        value_three = value_doc.reshape(SEQ, KVH, HD)

        def per_head(head_number):
            group_number = head_number // GROUP
            query_head = lax.dynamic_index_in_dim(query_three, head_number, 1, keepdims=False)
            grad_head = lax.dynamic_index_in_dim(grad_three, head_number, 1, keepdims=False)
            key_head = lax.dynamic_index_in_dim(key_three, group_number, 1, keepdims=False)
            value_head = lax.dynamic_index_in_dim(value_three, group_number, 1, keepdims=False)
            log_head = lax.dynamic_index_in_dim(log_doc, head_number, 0, keepdims=False)
            delta_head = lax.dynamic_index_in_dim(delta_doc, head_number, 0, keepdims=False)
            return attend_head(query_head, key_head, value_head, grad_head, log_head, delta_head, first_pos)

        grad_query = lax.map(per_head, jnp.arange(HEADS, dtype=jnp.int32))
        hashed_grads = jnp.einsum("hsd,hdb->shb", grad_query.astype(jnp.float32), table_out,
                                  precision=lax.Precision.HIGHEST).astype(jnp.bfloat16)
        hashed_inputs = jnp.dot(input_doc, table_in.astype(jnp.bfloat16),
                                preferred_element_type=jnp.float32).astype(jnp.bfloat16)
        sketch = jnp.einsum("sa,shb->ab", hashed_inputs.astype(jnp.float32), hashed_grads.astype(jnp.float32),
                            precision=lax.Precision.HIGHEST)
        return (sketch * (SEQ * D // K1) ** -0.5).reshape(SK)

    doc_sketch = lax.map(one_document, (queries, key_heads, value_heads, out_grad, log_sums, row_delta, doc_start, layer_input))
    scores = jnp.dot(doc_sketch, query_sketch.astype(jnp.float32).T, precision=lax.Precision.HIGHEST) * SK ** -0.5
    return doc_sketch, scores
```

```python
import functools

import jax
import jax.numpy as jnp
from jax import lax
from jax.experimental import pallas as pl
from jax.experimental.pallas import tpu as pltpu
from jax.sharding import PartitionSpec as P

HD = 128
K1 = 128
K2 = 64
LANES = 128
VMEM_LIMIT = 48 * 1024 * 1024


def dot_nt(left, right):
    return lax.dot_general(
        left, right, (((1,), (1,)), ((), ())), preferred_element_type=jnp.float32
    )


def dot_tn(left, right):
    return lax.dot_general(
        left, right, (((0,), (0,)), ((), ())), preferred_element_type=jnp.float32
    )


def sign_table(codes, levels, buckets):
    plus_part = (codes[:, None] == levels[None, :]).astype(jnp.float32)
    minus_part = (codes[:, None] == levels[None, :] + buckets).astype(jnp.float32)
    return (plus_part - minus_part).astype(jnp.bfloat16)


def split_terms(value, terms):
    parts = []
    for _ in range(terms):
        part = value.astype(jnp.bfloat16)
        parts.append(part)
        value = value - part.astype(jnp.float32)
    return parts


def stage_kernel(info, *refs, heads, causal, first, last, scale):
    refs = list(refs)
    q_own, q_sib, g_own, g_sib, log_ref, delta_ref, table_ref = refs[:7]
    k_same, k_cross, v_same, v_cross = refs[7:11]
    rest = refs[11:]
    if not first:
        before = rest.pop(0)
    if last:
        hi_own, hi_sib = rest.pop(0), rest.pop(0)
    out_ref, total = rest
    group = pl.program_id(0)
    rows = q_own.shape[0]
    keys = jnp.concatenate([k_same[...], k_cross[...]], axis=0)
    values = jnp.concatenate([v_same[...], v_cross[...]], axis=0)
    key_index = lax.broadcasted_iota(jnp.int32, (2 * rows, LANES), 0)
    key_pos = jnp.where(key_index < rows, info[4] + key_index, info[5] - rows + key_index)
    seen = key_pos >= info[3]
    if causal:
        shape = (2 * rows, 2 * rows)
        row_at = lax.broadcasted_iota(jnp.int32, shape, 0)
        col_at = lax.broadcasted_iota(jnp.int32, shape, 1)
        row_at = jnp.where(row_at < rows, info[1] + row_at, info[2] - rows + row_at)
        col_at = jnp.where(col_at < rows, info[4] + col_at, info[5] - rows + col_at)
        visible = col_at <= row_at
    log_cols = log_ref[...].T
    delta_cols = delta_ref[...].T

    @pl.when(group == 0)
    def _():
        if first:
            total[...] = jnp.zeros_like(total)
        else:
            total[...] = before[...]

    sums = jnp.zeros(total.shape, jnp.float32)
    for head in range(heads):
        at = slice(head * HD, (head + 1) * HD)
        hashed_keys = jnp.dot(keys, table_ref[at, :], preferred_element_type=jnp.float32)
        hashed_keys = jnp.where(seen, hashed_keys, 0.0).astype(jnp.bfloat16)
        query = jnp.concatenate([q_own[:, at], q_sib[:, at]], axis=0)
        grad = jnp.concatenate([g_own[:, at], g_sib[:, at]], axis=0)
        logits = dot_nt(query, keys) * (HD**-0.5) - log_cols[:, head : head + 1]
        weights = jnp.exp(jnp.minimum(logits, 1.0))
        if causal:
            weights = jnp.where(visible, weights, 0.0)
        grad_weights = dot_nt(grad, values) - delta_cols[:, head : head + 1]
        scores = (weights * grad_weights).astype(jnp.bfloat16)
        sums += jnp.dot(scores, hashed_keys, preferred_element_type=jnp.float32)
    total[...] += sums

    @pl.when(group == pl.num_programs(0) - 1)
    def _():
        if not last:
            out_ref[...] = total[...]
        else:
            hashed = jnp.concatenate([hi_own[...], hi_sib[...]], axis=0)
            both = sum(dot_tn(hashed, part) for part in split_terms(total[...], 2))
            half = K1 // 2
            lane = lax.broadcasted_iota(jnp.int32, (half, LANES), 1)
            out_ref[...] = jnp.where(lane < K2, both[:half], both[half:]) * scale


def stage(info, q, q_sib, g, g_sib, logs, deltas, table, same, cross, before, hashed, causal, scale):
    rows = q.shape[0]
    half = q_sib.shape[1]
    groups = same.shape[1] // (2 * HD)
    width = half // groups
    heads = width // HD
    first, last = before is None, hashed is not None
    own_spec = pl.BlockSpec((rows, width), lambda g, info: (0, info[0] * groups + g))
    sib_spec = pl.BlockSpec((rows, width), lambda g, info: (0, g))
    stat_spec = pl.BlockSpec((heads, 2 * rows), lambda g, info: (g, 0))
    key_spec = pl.BlockSpec((rows, HD), lambda g, info: (0, g))
    value_spec = pl.BlockSpec((rows, HD), lambda g, info: (0, groups + g))
    whole = lambda shape: pl.BlockSpec(shape, lambda g, info: (0, 0))
    in_specs = [own_spec, sib_spec, own_spec, sib_spec, stat_spec, stat_spec]
    in_specs += [pl.BlockSpec((width, LANES), lambda g, info: (g, 0))]
    in_specs += [key_spec, key_spec, value_spec, value_spec]
    args = [q, q_sib, g, g_sib, logs, deltas, table, same, cross, same, cross]
    if not first:
        in_specs.append(whole(before.shape))
        args.append(before)
    if last:
        in_specs += [whole(hashed[0].shape)] * 2
        args += list(hashed)
    out_shape = (K1 // 2, LANES) if last else (2 * rows, LANES)
    cells = 2 * rows * 2 * rows * heads * groups
    return pl.pallas_call(
        functools.partial(
            stage_kernel, heads=heads, causal=causal, first=first, last=last, scale=scale
        ),
        out_shape=jax.ShapeDtypeStruct(out_shape, jnp.float32),
        grid_spec=pltpu.PrefetchScalarGridSpec(
            num_scalar_prefetch=1,
            grid=(groups,),
            in_specs=in_specs,
            out_specs=whole(out_shape),
            scratch_shapes=[pltpu.VMEM((2 * rows, LANES), jnp.float32)],
        ),
        compiler_params=pltpu.CompilerParams(vmem_limit_bytes=VMEM_LIMIT),
        cost_estimate=pl.CostEstimate(
            flops=6 * HD * cells, bytes_accessed=5 * 2**20, transcendentals=cells
        ),
    )(info, *args)


def score_kernel(info, recv_ref, stored_ref, own_ref, partial_ref, sums, flat, *, scale):
    docs, parts, chunk, _ = recv_ref.shape
    for doc in range(docs):
        sums[doc] = jnp.sum(recv_ref[doc], axis=0)
    for row in range(chunk):
        flat[:, row * LANES : (row + 1) * LANES] = sums[:, row, :]
        own_ref[:, row * LANES : (row + 1) * LANES] = sums[info[0], row : row + 1, :]
    pieces = split_terms(flat[...], 3)
    stacked = jnp.concatenate(pieces, axis=0)
    products = dot_nt(stacked, stored_ref[...])
    partial = (products[:docs] + products[docs : 2 * docs] + products[2 * docs :]) * scale
    if len(partial_ref.shape) == 3:
        for part in range(parts):
            partial_ref[part] = partial[:, part * LANES : (part + 1) * LANES]
    else:
        partial_ref[...] = partial


def local(
    queries,
    key_heads,
    value_heads,
    out_grad,
    log_sums,
    row_delta,
    doc_start,
    layer_input,
    hash_in,
    hash_out,
    query_sketch,
):
    ctx_count = lax.axis_size("ctx")
    docs = lax.axis_size("doc")
    chips = ctx_count // 2
    place = lax.axis_index("ctx")
    chip, core = place // 2, place % 2
    tok_rows = queries.shape[1]
    seq_len = tok_rows * ctx_count
    local_heads = log_sums.shape[1]
    core_heads = local_heads * chips
    half = queries.shape[2] // 2
    kv_half = key_heads.shape[2] // 2
    first_core = core == 0

    def halves(array, width):
        low, high = array[:, :width], array[:, width:]
        return jnp.where(first_core, low, high), jnp.where(first_core, high, low)

    def permute(array, target):
        pairs = [(i, target(i)) for i in range(ctx_count)]
        return lax.ppermute(array, "ctx", [pair for pair in pairs if pair[1] < ctx_count])

    key_mine, key_other = halves(key_heads[0], kv_half)
    value_mine, value_other = halves(value_heads[0], kv_half)
    mine = jnp.concatenate([key_mine, value_mine], axis=1)
    other = jnp.concatenate([key_other, value_other], axis=1)
    arrived = {}
    for step in range(chips - 1, 0, -1):
        arrived[step] = (
            permute(mine, lambda i: i + 2 * step),
            permute(other, lambda i: (i ^ 1) + 2 * step),
        )
    swap = lambda array: permute(array, lambda i: i ^ 1)
    arrived[0] = (mine, swap(other))
    q_sib = swap(halves(queries[0], half)[1])
    g_sib = swap(halves(out_grad[0], half)[1])

    stats = jnp.concatenate([log_sums[0], row_delta[0]], axis=0)
    stats = stats.reshape(2 * local_heads, chips, 2 * tok_rows).transpose(1, 0, 2)
    codes = hash_out.astype(jnp.float32).reshape(1, -1, 2 * tok_rows) if (
        hash_out.shape[0] % (2 * tok_rows) == 0
    ) else jnp.pad(hash_out.astype(jnp.float32), (0, -hash_out.shape[0] % (2 * tok_rows))).reshape(
        1, -1, 2 * tok_rows
    )
    code_rows = codes.shape[1]
    packed = jnp.concatenate(
        [stats, jnp.broadcast_to(codes, (chips, code_rows, 2 * tok_rows))], axis=1
    )
    packed = jnp.broadcast_to(packed[:, None], (chips, 2) + packed.shape[1:]).reshape(
        (ctx_count,) + packed.shape[1:]
    )
    packed = lax.all_to_all(packed, "ctx", split_axis=0, concat_axis=0, tiled=True)
    packed = jnp.where(first_core, packed[:chips], packed[chips:])
    stats = packed[:, : 2 * local_heads]
    stats = jnp.where(
        first_core,
        stats,
        jnp.concatenate([stats[:, :, tok_rows:], stats[:, :, :tok_rows]], axis=2),
    )
    logs = stats[:, :local_heads].reshape(core_heads, 2 * tok_rows)
    deltas = stats[:, local_heads:].reshape(core_heads, 2 * tok_rows)
    codes = packed[:, 2 * local_heads :].reshape(chips, -1)[:, : local_heads * HD]
    out_levels = (jnp.arange(LANES, dtype=jnp.int32) % K2).astype(jnp.float32)
    table_out = sign_table(codes.reshape(-1), out_levels, float(K2))

    in_levels = jnp.arange(K1, dtype=jnp.int32)
    in_levels = (in_levels % (K1 // 2)) * 2 + in_levels // (K1 // 2)
    table_in = sign_table(hash_in, in_levels, K1)
    hashed = jnp.dot(layer_input[0], table_in, preferred_element_type=jnp.float32).astype(
        jnp.bfloat16
    )
    hashed_pair = (hashed, swap(hashed))

    own_base = place * tok_rows
    sib_base = (place ^ 1) * tok_rows
    scale = HD**-0.5 * (seq_len * layer_input.shape[2] // K1) ** -0.5
    total = None
    for step in range(chips):
        shift = 2 * step * tok_rows
        info = jnp.stack(
            [core, own_base, sib_base, doc_start[0], own_base - shift, sib_base - shift]
        ).astype(jnp.int32)
        total = stage(
            info,
            queries[0],
            q_sib,
            out_grad[0],
            g_sib,
            logs,
            deltas,
            table_out,
            arrived[step][0],
            arrived[step][1],
            total,
            hashed_pair if step == chips - 1 else None,
            step == 0,
            scale,
        )

    chunk = K1 * K2 // LANES // ctx_count
    parts = total.reshape(1, ctx_count, chunk, LANES)
    parts = jnp.broadcast_to(parts, (docs,) + parts.shape[1:]).reshape(-1, chunk, LANES)
    parts = lax.all_to_all(parts, ("doc", "ctx"), split_axis=0, concat_axis=0, tiled=True)
    parts = parts.reshape(docs, ctx_count, chunk, LANES)
    stored = query_sketch.shape[0]
    wide = stored // ctx_count == LANES
    partial_shape = (ctx_count, docs, LANES) if wide else (docs, stored)
    local_sketch, partial = pl.pallas_call(
        functools.partial(score_kernel, scale=(K1 * K2) ** -0.5),
        out_shape=(
            jax.ShapeDtypeStruct((1, chunk * LANES), jnp.float32),
            jax.ShapeDtypeStruct(partial_shape, jnp.float32),
        ),
        in_specs=[
            pl.BlockSpec(memory_space=pltpu.SMEM),
            pl.BlockSpec(memory_space=pltpu.VMEM),
            pl.BlockSpec(memory_space=pltpu.VMEM),
        ],
        out_specs=(
            pl.BlockSpec(memory_space=pltpu.VMEM),
            pl.BlockSpec(memory_space=pltpu.VMEM),
        ),
        scratch_shapes=[
            pltpu.VMEM((docs, chunk, LANES), jnp.float32),
            pltpu.VMEM((docs, chunk * LANES), jnp.float32),
        ],
        compiler_params=pltpu.CompilerParams(vmem_limit_bytes=VMEM_LIMIT),
    )(lax.axis_index("doc").astype(jnp.int32).reshape(1), parts, query_sketch)
    if not wide:
        partial = partial.reshape(docs, ctx_count, -1).transpose(1, 0, 2)
    partial = lax.all_to_all(partial, "ctx", split_axis=0, concat_axis=0, tiled=True)
    return local_sketch, jnp.sum(partial, axis=0)


def solution(mesh):
    return jax.shard_map(
        local,
        mesh=mesh,
        in_specs=(
            P("doc", "ctx", None),
            P("doc", "ctx", None),
            P("doc", "ctx", None),
            P("doc", "ctx", None),
            P("doc", "ctx", None),
            P("doc", "ctx", None),
            P("doc"),
            P("doc", "ctx", None),
            P(),
            P("ctx"),
            P("doc", "ctx"),
        ),
        out_specs=(P("doc", "ctx"), P(None, ("doc", "ctx"))),
        check_vma=False,
    )
```

```python
import functools

import jax
import jax.numpy as jnp
from jax import lax
from jax.experimental import pallas as pl
from jax.experimental.pallas import tpu as pltpu
from jax.sharding import PartitionSpec as P

HD = 128
K1 = 128
K2 = 64
LANES = 128
FACTOR = HD**-0.5
STAT_TERMS = 3
NO_STEP = 1024
MIB = 1024 * 1024
SMEM = pl.BlockSpec(memory_space=pltpu.SMEM)
VMEM = pl.BlockSpec(memory_space=pltpu.VMEM)
ANY = pl.BlockSpec(memory_space=pl.ANY)


def dot_nt(left, right):
    return lax.dot_general(
        left, right, (((1,), (1,)), ((), ())), preferred_element_type=jnp.float32
    )


def dot_tn(left, right):
    return lax.dot_general(
        left, right, (((0,), (0,)), ((), ())), preferred_element_type=jnp.float32
    )


def split_terms(value, terms):
    parts = []
    for _ in range(terms):
        part = value.astype(jnp.bfloat16)
        parts.append(part)
        value = value - part.astype(jnp.float32)
    return parts


def fetch(pairs, sems):
    copies = [
        pltpu.make_async_copy(source, target, sems.at[index])
        for index, (source, target) in enumerate(pairs)
    ]
    for copy in copies:
        copy.start()
    return copies


def pack_kernel(logs_in, deltas_in, codes_in, packed, logs, deltas, codes, sems):
    for copy in fetch(((logs_in, logs), (deltas_in, deltas), (codes_in, codes)), sems):
        copy.wait()
    heads = logs.shape[0]
    code_rows = codes[...].astype(jnp.float32)
    for target in range(packed.shape[0]):
        own = slice(target * LANES, (target + 1) * LANES)
        sib = slice((target ^ 1) * LANES, ((target ^ 1) + 1) * LANES)
        packed[target, :heads, :] = logs[:, own]
        packed[target, heads : 2 * heads, :] = logs[:, sib]
        packed[target, 2 * heads : 3 * heads, :] = deltas[:, own]
        packed[target, 3 * heads : 4 * heads, :] = deltas[:, sib]
        packed[target, 4 * heads :, :] = code_rows


def prepare_kernel(place, key_in, value_in, mine, other, key, value, sems):
    rows = key.shape[0] // 2
    pieces = [pl.ds(low, rows) for low in (0, rows)]
    for copy in fetch(
        [
            (source.at[piece, :], target.at[piece, :])
            for piece in pieces
            for source, target in ((key_in, key), (value_in, value))
        ],
        sems,
    ):
        copy.wait()
    core = place[0] % 2
    half = key.shape[1] // 2
    for at_core in range(2):

        @pl.when(core == at_core)
        def _(at_core=at_core):
            near = slice(at_core * half, (at_core + 1) * half)
            far = slice((1 - at_core) * half, (2 - at_core) * half)
            mine[:, :half], mine[:, half:] = key[:, near], value[:, near]
            other[:, :half], other[:, half:] = key[:, far], value[:, far]


def join_kernel(upper, lower, _, out, sems):
    rows = upper.shape[0]
    targets = (out.at[pl.ds(0, rows), :], out.at[pl.ds(rows, rows), :])
    for copy in fetch(zip((upper, lower), targets), sems):
        copy.wait()


def hash_kernel(rows_in, codes_in, _, out, rows, codes, sems):
    count, _, width = rows.shape
    pairs = [(codes_in, codes)]
    for part in range(count):
        pairs.append((rows_in.at[:, pl.ds(part * width, width)], rows.at[part]))
    copies = fetch(pairs, sems)
    copies[0].wait()
    level = lax.broadcasted_iota(jnp.int32, (K1, width), 0)
    level = jnp.where(level < K1 // 2, 2 * level, 2 * level - K1 + 1)
    total = jnp.zeros(out.shape, jnp.float32)
    for part in range(count):
        code = codes[:, part * width : (part + 1) * width]
        sign = jnp.where(code >= K1, -1.0, 1.0)
        bucket = jnp.where(code >= K1, code - K1, code)
        table = jnp.where(level == bucket, sign, 0.0).astype(jnp.bfloat16)
        copies[1 + part].wait()
        total += dot_nt(rows[part], table)
    out[...] = total.astype(out.dtype)


def relay_kernel(place, pair, received, _, out, sems, *, relaying):
    chip = place[0] // 2
    passing = functools.reduce(jnp.logical_or, [chip == which for which in relaying])

    @pl.when(passing)
    def _():
        fetch([(received, out)], sems)[0].wait()

    @pl.when(jnp.logical_not(passing))
    def _():
        fetch([(pair, out)], sems)[0].wait()


def attend(place, start, q_at, g_at, tables, pairs, steps, causal, group, kv_groups, total):
    core = place[0] % 2
    rows = total.shape[0]
    half = rows // 2
    count = q_at.shape[0] // rows
    own_base = place[0] * half
    sib_base = jnp.where(core == 0, own_base + half, own_base - half)
    index = lax.broadcasted_iota(jnp.int32, (rows, LANES), 0)
    spread = jnp.where(index < half, own_base + index, sib_base - half + index)
    lane = lax.broadcasted_iota(jnp.int32, (rows, LANES), 1)
    ones = jnp.where(lane < STAT_TERMS * count, 1.0, 0.0).astype(jnp.bfloat16)
    keys, key_sides, value_sides = [], [], []
    for pair, step in zip(pairs, steps):
        at = slice(group * HD, (group + 1) * HD)
        seen = spread - step * rows >= start[0]
        keys.append(jnp.where(seen, pair[:, at], jnp.zeros((), jnp.bfloat16)))
        at = slice((kv_groups + group) * HD, (kv_groups + group + 1) * HD)
        key_sides.append(jnp.concatenate([keys[-1], ones], axis=1))
        value_sides.append(jnp.concatenate([pair[:, at], ones], axis=1))
    if causal:
        shape = (rows, rows)
        row_at = lax.broadcasted_iota(jnp.int32, shape, 0)
        col_at = lax.broadcasted_iota(jnp.int32, shape, 1)
        row_at = jnp.where(row_at < half, own_base + row_at, sib_base - half + row_at)
        col_at = jnp.where(col_at < half, own_base + col_at, sib_base - half + col_at)
        visible = (col_at <= row_at)[None]
    parts = 2 if count % 2 == 0 else 1
    size = count * rows // parts
    hashed = []
    for part in range(parts):
        at = pl.ds(part * size, size)
        grads = None
        for key, key_side, value_side in zip(keys, key_sides, value_sides):
            logits = dot_nt(q_at[at, :], key_side) * FACTOR
            weights = jnp.exp(jnp.minimum(logits, 1.0))
            if causal and key is keys[0]:
                weights = weights.reshape(count // parts, rows, rows)
                weights = jnp.where(visible, weights, 0.0).reshape(size, rows)
            scores = (weights * dot_nt(g_at[at, :], value_side)).astype(jnp.bfloat16)
            product = jnp.dot(scores, key, preferred_element_type=jnp.float32)
            grads = product if grads is None else grads + product
        grads = (grads * FACTOR).astype(jnp.bfloat16)
        hashed += [grads[low : low + rows] for low in range(0, size, rows)]
    hashed = jnp.concatenate(hashed, axis=1)
    total[...] += jnp.dot(hashed, tables[...], preferred_element_type=jnp.float32)


def first_kernel(place, start, q, q_sib, g, g_sib, stats, pair_in, *refs):
    total, q_all, g_all, tables, pair, sems, pair_sem = refs
    pair_copy = fetch([(pair_in, pair)], pair_sem)[0]
    core = place[0] % 2
    rows = total.shape[0]
    half = rows // 2
    kv_groups = pair.shape[1] // (2 * HD)
    heads = q_all.shape[0] // rows
    count = heads // kv_groups
    local_heads = stats.shape[1] // 5
    chips = stats.shape[0] // 2
    for group in range(kv_groups):
        for head in range(group * count, (group + 1) * count):
            column = pl.multiple_of((core * heads + head) * HD, HD)
            for which, (own, sib, out) in enumerate(((q, q_sib, q_all), (g, g_sib, g_all))):
                for source, low in ((own, head * rows), (sib, head * rows + half)):
                    pltpu.make_async_copy(
                        source.at[:, pl.ds(column, HD)],
                        out.at[pl.ds(low, half), pl.ds(0, HD)],
                        sems.at[group, which],
                    ).start()

    def stat_rows(which, group):
        found = []
        for head in range(group * count, (group + 1) * count):
            source, local = divmod(head, local_heads)
            row = which * local_heads + local
            found.append(stats[core * chips + source, row : row + 1, :])
        return jnp.concatenate(found, axis=0)

    total[...] = jnp.zeros_like(total)
    lane = lax.broadcasted_iota(jnp.int32, (half, LANES), 1)
    level = lax.broadcasted_iota(jnp.int32, (LANES, HD), 0)
    level = jnp.where(level < K2, level, level - K2).astype(jnp.float32)
    for group in range(kv_groups):
        for out, base, sign in ((q_all, 0, -1.0 / FACTOR), (g_all, 2, -1.0)):
            for side in range(2):
                terms = split_terms(stat_rows(base + side, group) * sign, STAT_TERMS)
                terms = jnp.concatenate([term.astype(jnp.float32) for term in terms], axis=0)
                fill = jnp.zeros((LANES - terms.shape[0], half), jnp.float32)
                columns = jnp.concatenate([terms, fill], axis=0).T
                for head in range(count):
                    chosen = jnp.where(lane % count == head, columns, 0.0)
                    low = (group * count + head) * rows + side * half
                    out[low : low + half, HD:] = chosen.astype(jnp.bfloat16)
        codes = stat_rows(4, group)
        for head in range(count):
            code = codes[head : head + 1]
            sign = jnp.where(code >= K2, -1.0, 1.0)
            bucket = jnp.where(code >= K2, code - K2, code)
            table = jnp.where(level == bucket, sign, 0.0)
            low = (group * count + head) * HD
            tables[low : low + HD, :] = table.T.astype(jnp.bfloat16)
    pair_copy.wait()
    for group in range(kv_groups):
        at = pl.ds(group * count * rows, count * rows)
        for which, out in enumerate((q_all, g_all)):
            side = out.at[at, pl.ds(0, HD)]
            pltpu.make_async_copy(side, side, sems.at[group, which]).wait()
        attend(
            place, start, q_all.at[at, :], g_all.at[at, :],
            tables.at[pl.ds(group * count * HD, count * HD), :],
            [pair], [0], True, group, kv_groups, total,
        )


def next_kernel(place, start, q_all, g_all, tables, before, pair, total, *, steps):
    rows = total.shape[0]
    kv_groups = pair.shape[1] // (2 * HD)
    size = q_all.shape[0] // kv_groups
    width = tables.shape[0] // kv_groups
    chip = place[0] // 2
    step = jnp.int32(NO_STEP)
    for at_chip, known in steps.items():
        step = jnp.where(chip == at_chip, known, step)
    total[...] = before[...]
    for group in range(kv_groups):
        at = pl.ds(group * size, size)
        attend(
            place, start, q_all.at[at, :], g_all.at[at, :],
            tables.at[pl.ds(group * width, width), :],
            [pair], [step], False, group, kv_groups, total,
        )


def last_kernel(
    place, start, q_all, g_all, tables, before, pair, hi_own, hi_sib, out, total, *, steps, scale
):
    next_kernel(place, start, q_all, g_all, tables, before, pair, total, steps=steps)
    hashed = jnp.concatenate([hi_own[...], hi_sib[...]], axis=0)
    both = sum(dot_tn(hashed, part) for part in split_terms(total[...], 2))
    half = K1 // 2
    lane = lax.broadcasted_iota(jnp.int32, (half, LANES), 1)
    sketch = jnp.where(lane < K2, both[:half], both[half:]) * scale
    parts, chunk = out.shape[1], out.shape[2]
    for part in range(parts):
        for doc in range(out.shape[0]):
            out[doc, part] = sketch[part * chunk : (part + 1) * chunk]


def score_kernel(place, recv_ref, stored_ref, own_ref, partial_ref, sums, flat, *, scale):
    docs, parts, chunk, _ = recv_ref.shape
    for doc in range(docs):
        sums[doc] = jnp.sum(recv_ref[doc], axis=0)
    for row in range(chunk):
        flat[:, row * LANES : (row + 1) * LANES] = sums[:, row, :]
        own_ref[:, row * LANES : (row + 1) * LANES] = sums[place[0], row : row + 1, :]
    pieces = split_terms(flat[...], 3)
    stacked = jnp.concatenate(pieces, axis=0)
    products = dot_nt(stacked, stored_ref[...])
    partial = (products[:docs] + products[docs : 2 * docs] + products[2 * docs :]) * scale
    if len(partial_ref.shape) == 3:
        for part in range(parts):
            partial_ref[part] = partial[:, part * LANES : (part + 1) * LANES]
    else:
        partial_ref[...] = partial


def local(
    queries,
    key_heads,
    value_heads,
    out_grad,
    log_sums,
    row_delta,
    doc_start,
    layer_input,
    hash_in,
    hash_out,
    query_sketch,
):
    ctx_count = lax.axis_size("ctx")
    docs = lax.axis_size("doc")
    chips = ctx_count // 2
    place = lax.axis_index("ctx").astype(jnp.int32).reshape(1)
    doc_place = lax.axis_index("doc").astype(jnp.int32).reshape(1)
    rows = queries.shape[1]
    seq_len = rows * ctx_count
    local_heads = log_sums.shape[1]
    core_heads = local_heads * chips
    kv_width = key_heads.shape[2]
    shape = jax.ShapeDtypeStruct
    params = lambda mib: pltpu.CompilerParams(vmem_limit_bytes=mib * MIB)

    def permute(array, target):
        pairs = [(i, target(i)) for i in range(ctx_count)]
        return lax.ppermute(array, "ctx", [pair for pair in pairs if pair[1] < ctx_count])

    swap = lambda array: permute(array, lambda i: i ^ 1)

    packed_shape = (ctx_count, 5 * local_heads, LANES)
    packed = pl.pallas_call(
        pack_kernel,
        out_shape=shape(packed_shape, jnp.float32),
        in_specs=[ANY] * 3,
        out_specs=VMEM,
        scratch_shapes=[
            pltpu.VMEM((local_heads, seq_len), jnp.float32),
            pltpu.VMEM((local_heads, seq_len), jnp.float32),
            pltpu.VMEM((local_heads, HD), jnp.int32),
            pltpu.SemaphoreType.DMA((3,)),
        ],
        compiler_params=params(60),
    )(log_sums[0], row_delta[0], hash_out.reshape(local_heads, HD))
    stats = lax.all_to_all(packed, "ctx", split_axis=0, concat_axis=0, tiled=True)
    half_shape = shape((rows, kv_width), jnp.bfloat16)
    mine, other = pl.pallas_call(
        prepare_kernel,
        out_shape=(half_shape, half_shape),
        in_specs=[SMEM, ANY, ANY],
        out_specs=(VMEM, VMEM),
        scratch_shapes=[pltpu.VMEM((rows, kv_width), jnp.bfloat16)] * 2
        + [pltpu.SemaphoreType.DMA((4,))],
        compiler_params=params(60),
    )(place, key_heads[0], value_heads[0])
    from_sib = swap(other)

    pair_shape = shape((2 * rows, kv_width), jnp.bfloat16)
    pair = pl.pallas_call(
        join_kernel,
        out_shape=pair_shape,
        in_specs=[ANY] * 3,
        out_specs=VMEM,
        scratch_shapes=[pltpu.SemaphoreType.DMA((2,))],
        compiler_params=params(16),
    )(mine, from_sib, stats)

    if chips == 4:
        plan = [
            [(0, 2, 2), (2, 3, 1)],
            [(1, 3, 2), (0, 1, 1)],
            [(2, 3, 3), (1, 2, 1)],
        ]
    else:
        plan = [
            [(chip, chip + 1, wave + 1) for chip in range(wave, chips - 1)]
            for wave in range(chips - 1)
        ]

    def send(block, wave):
        route = {low: high for low, high, _ in plan[wave]}
        return permute(block, lambda i: 2 * route.get(i // 2, chips) + i % 2)

    received = [send(pair, 0)]
    if chips == 4:
        received.append(send(pair, 1))
    q, g = queries[0], out_grad[0]
    q_sib, g_sib = swap(q), swap(g)


    stacked = shape((core_heads * 2 * rows, 2 * HD), jnp.bfloat16)
    table_shape = shape((core_heads * HD, LANES), jnp.bfloat16)
    total_shape = shape((2 * rows, LANES), jnp.float32)
    total, q_all, g_all, tables = pl.pallas_call(
        first_kernel,
        out_shape=(total_shape, stacked, stacked, table_shape),
        in_specs=[SMEM, SMEM, ANY, ANY, ANY, ANY, VMEM, ANY],
        out_specs=(VMEM, VMEM, VMEM, VMEM),
        scratch_shapes=[
            pltpu.VMEM((2 * rows, kv_width), jnp.bfloat16),
            pltpu.SemaphoreType.DMA((kv_width // (2 * HD), 2)),
            pltpu.SemaphoreType.DMA((1,)),
        ],
        compiler_params=params(24),
    )(place, doc_start, q, q_sib, g, g_sib, stats, pair)

    parts = max(1, layer_input.shape[2] // 1024)
    width = layer_input.shape[2] // parts
    hashed = pl.pallas_call(
        hash_kernel,
        out_shape=shape((rows, K1), jnp.bfloat16),
        in_specs=[ANY, ANY, ANY],
        out_specs=VMEM,
        scratch_shapes=[
            pltpu.VMEM((parts, rows, width), jnp.bfloat16),
            pltpu.VMEM((1, parts * width), jnp.int32),
            pltpu.SemaphoreType.DMA((1 + parts,)),
        ],
        compiler_params=params(16),
    )(layer_input[0], hash_in.reshape(1, -1), total)
    hashed_sib = swap(hashed)

    scale = (seq_len * layer_input.shape[2] // K1) ** -0.5
    chunk = K1 * K2 // LANES // ctx_count
    if chips == 4:
        relayed = pl.pallas_call(
            functools.partial(relay_kernel, relaying=[2]),
            out_shape=pair_shape,
            in_specs=[SMEM] + [ANY] * 3,
            out_specs=VMEM,
            scratch_shapes=[pltpu.SemaphoreType.DMA((1,))],
            compiler_params=params(16),
        )(place, pair, received[0], total)
        received.append(send(relayed, 2))
    for wave in range(len(received), len(plan)):
        received.append(send(received[-1], wave))

    for wave, block in enumerate(received):
        steps = {high: step for _, high, step in plan[wave]}
        last = wave == len(plan) - 1
        args = (place, doc_start, q_all, g_all, tables, total, block)
        if not last:
            total = pl.pallas_call(
                functools.partial(next_kernel, steps=steps),
                out_shape=total_shape,
                in_specs=[SMEM, SMEM] + [VMEM] * 5,
                out_specs=VMEM,
                compiler_params=params(24),
            )(*args)
            continue
        parts = pl.pallas_call(
            functools.partial(last_kernel, steps=steps, scale=scale),
            out_shape=shape((docs, ctx_count, chunk, LANES), jnp.float32),
            in_specs=[SMEM, SMEM] + [VMEM] * 7,
            out_specs=VMEM,
            scratch_shapes=[pltpu.VMEM((2 * rows, LANES), jnp.float32)],
            compiler_params=params(24),
        )(*args, hashed, hashed_sib)

    parts = parts.reshape(-1, chunk, LANES)
    parts = lax.all_to_all(parts, ("doc", "ctx"), split_axis=0, concat_axis=0, tiled=True)
    parts = parts.reshape(docs, ctx_count, chunk, LANES)
    stored = query_sketch.shape[0]
    wide = stored // ctx_count == LANES
    partial_shape = (ctx_count, docs, LANES) if wide else (docs, stored)
    local_sketch, partial = pl.pallas_call(
        functools.partial(score_kernel, scale=(K1 * K2) ** -0.5),
        out_shape=(
            shape((1, chunk * LANES), jnp.float32),
            shape(partial_shape, jnp.float32),
        ),
        in_specs=[SMEM, VMEM, VMEM],
        out_specs=(VMEM, VMEM),
        scratch_shapes=[
            pltpu.VMEM((docs, chunk, LANES), jnp.float32),
            pltpu.VMEM((docs, chunk * LANES), jnp.float32),
        ],
        compiler_params=params(16),
    )(doc_place, parts, query_sketch)
    if not wide:
        partial = partial.reshape(docs, ctx_count, -1).transpose(1, 0, 2)
    partial = lax.all_to_all(partial, "ctx", split_axis=0, concat_axis=0, tiled=True)
    return local_sketch, jnp.sum(partial, axis=0)


def solution(mesh):
    return jax.shard_map(
        local,
        mesh=mesh,
        in_specs=(
            P("doc", "ctx", None),
            P("doc", "ctx", None),
            P("doc", "ctx", None),
            P("doc", "ctx", None),
            P("doc", "ctx", None),
            P("doc", "ctx", None),
            P("doc"),
            P("doc", "ctx", None),
            P(),
            P("ctx"),
            P("doc", "ctx"),
        ),
        out_specs=(P("doc", "ctx"), P(None, ("doc", "ctx"))),
        check_vma=False,
    )
```

```python
import functools

import jax
import jax.numpy as jnp
from jax import lax
from jax.experimental import pallas as pl
from jax.experimental.pallas import tpu as pltpu
from jax.sharding import PartitionSpec as P

HD = 128
K1 = 128
K2 = 64
LANES = 128
FACTOR = HD**-0.5
STAT_TERMS = 3
NO_STEP = 1024
GROUP = 8
MIB = 1024 * 1024
SMEM = pl.BlockSpec(memory_space=pltpu.SMEM)
VMEM = pl.BlockSpec(memory_space=pltpu.VMEM)
ANY = pl.BlockSpec(memory_space=pl.ANY)


def dot_nt(left, right):
    return lax.dot_general(
        left, right, (((1,), (1,)), ((), ())), preferred_element_type=jnp.float32
    )


def dot_tn(left, right):
    return lax.dot_general(
        left, right, (((0,), (0,)), ((), ())), preferred_element_type=jnp.float32
    )


def split_terms(value, terms):
    parts = []
    for _ in range(terms):
        part = value.astype(jnp.bfloat16)
        parts.append(part)
        value = value - part.astype(jnp.float32)
    return parts


def fetch(pairs, sems):
    copies = [
        pltpu.make_async_copy(source, target, sems.at[index])
        for index, (source, target) in enumerate(pairs)
    ]
    for copy in copies:
        copy.start()
    return copies


def pack_kernel(logs_in, deltas_in, codes_in, packed, logs, deltas, codes, sems):
    for copy in fetch(((logs_in, logs), (deltas_in, deltas), (codes_in, codes)), sems):
        copy.wait()
    heads = logs.shape[0]
    code_rows = codes[...].astype(jnp.float32)
    for target in range(packed.shape[0]):
        own = slice(target * LANES, (target + 1) * LANES)
        sib = slice((target ^ 1) * LANES, ((target ^ 1) + 1) * LANES)
        packed[target, :heads, :] = logs[:, own]
        packed[target, heads : 2 * heads, :] = logs[:, sib]
        packed[target, 2 * heads : 3 * heads, :] = deltas[:, own]
        packed[target, 3 * heads : 4 * heads, :] = deltas[:, sib]
        packed[target, 4 * heads :, :] = code_rows


def prepare_kernel(place, key_in, value_in, pair, other, key, value, mine, sems):
    rows = key.shape[0] // 2
    pieces = [pl.ds(low, rows) for low in (0, rows)]
    for copy in fetch(
        [
            (source.at[piece, :], target.at[piece, :])
            for piece in pieces
            for source, target in ((key_in, key), (value_in, value))
        ],
        sems,
    ):
        copy.wait()
    core = place[0] % 2
    half = key.shape[1] // 2
    for at_core in range(2):

        @pl.when(core == at_core)
        def _(at_core=at_core):
            near = slice(at_core * half, (at_core + 1) * half)
            far = slice((1 - at_core) * half, (2 - at_core) * half)
            mine[:, :half], mine[:, half:] = key[:, near], value[:, near]
            other[:, :half], other[:, half:] = key[:, far], value[:, far]

    for copy in fetch([(mine, pair.at[pl.ds(0, mine.shape[0]), :])], sems):
        copy.wait()


def join_kernel(_, lower, __, pair, *refs):
    parts, sems = refs[:-1], refs[-1]
    rows = lower.shape[0]
    copies = [(lower, pair.at[pl.ds(rows, rows), :])]
    for group, part in enumerate(parts):
        for half in range(2):
            at = pl.ds((half * len(parts) + group) * HD, HD)
            to = pl.ds(half * HD, HD)
            copies.append((pair.at[pl.ds(0, rows), at], part.at[pl.ds(0, rows), to]))
            copies.append((lower.at[:, at], part.at[pl.ds(rows, rows), to]))
    for copy in fetch(copies, sems):
        copy.wait()


def hash_kernel(rows_in, codes_in, out, rows, codes, sems):
    count, _, width = rows.shape
    pairs = [(codes_in, codes)]
    for part in range(count):
        pairs.append((rows_in.at[:, pl.ds(part * width, width)], rows.at[part]))
    copies = fetch(pairs, sems)
    copies[0].wait()
    level = lax.broadcasted_iota(jnp.int32, (K1, width), 0)
    level = jnp.where(level < K1 // 2, 2 * level, 2 * level - K1 + 1)
    total = jnp.zeros(out.shape, jnp.float32)
    for part in range(count):
        code = codes[:, part * width : (part + 1) * width]
        sign = jnp.where(code >= K1, -1.0, 1.0)
        bucket = jnp.where(code >= K1, code - K1, code)
        table = jnp.where(level == bucket, sign, 0.0).astype(jnp.bfloat16)
        copies[1 + part].wait()
        total += dot_nt(rows[part], table)
    out[...] = total.astype(out.dtype)


def attend(place, start, q_at, g_at, tables, blocks, steps, causal, total):
    core = place[0] % 2
    rows = total.shape[0]
    half = rows // 2
    count = q_at.shape[0] // rows
    own_base = place[0] * half
    sib_base = jnp.where(core == 0, own_base + half, own_base - half)
    index = lax.broadcasted_iota(jnp.int32, (rows, LANES), 0)
    spread = jnp.where(index < half, own_base + index, sib_base - half + index)
    lane = lax.broadcasted_iota(jnp.int32, (rows, LANES), 1)
    ones = jnp.where(lane < STAT_TERMS * count, 1.0, 0.0).astype(jnp.bfloat16)
    keys, key_sides, value_sides = [], [], []
    for block, step in zip(blocks, steps):
        seen = spread - step * rows >= start[0]
        keys.append(jnp.where(seen, block[:, :HD], jnp.zeros((), jnp.bfloat16)))
        key_sides.append(jnp.concatenate([keys[-1], ones], axis=1))
        value_sides.append(jnp.concatenate([block[:, HD:], ones], axis=1))
    if causal:
        shape = (rows, rows)
        row_at = lax.broadcasted_iota(jnp.int32, shape, 0)
        col_at = lax.broadcasted_iota(jnp.int32, shape, 1)
        row_at = jnp.where(row_at < half, own_base + row_at, sib_base - half + row_at)
        col_at = jnp.where(col_at < half, own_base + col_at, sib_base - half + col_at)
        visible = (col_at <= row_at)[None]
    parts = 2 if count % 2 == 0 else 1
    size = count * rows // parts
    hashed = []
    for part in range(parts):
        at = pl.ds(part * size, size)
        grads = None
        for key, key_side, value_side in zip(keys, key_sides, value_sides):
            logits = dot_nt(q_at[at, :], key_side) * FACTOR
            weights = jnp.exp(jnp.minimum(logits, 1.0))
            if causal and key is keys[0]:
                weights = weights.reshape(count // parts, rows, rows)
                weights = jnp.where(visible, weights, 0.0).reshape(size, rows)
            scores = (weights * dot_nt(g_at[at, :], value_side)).astype(jnp.bfloat16)
            product = jnp.dot(scores, key, preferred_element_type=jnp.float32)
            grads = product if grads is None else grads + product
        grads = (grads * FACTOR).astype(jnp.bfloat16)
        hashed += [grads[low : low + rows] for low in range(0, size, rows)]
    hashed = jnp.concatenate(hashed, axis=1)
    total[...] += jnp.dot(hashed, tables[...], preferred_element_type=jnp.float32)


def first_kernel(place, start, q, q_sib, g, g_sib, stats, pair_in, *refs):
    total, q_all, g_all, tables, pair, sems, pair_sem = refs
    pair_copy = fetch([(pair_in, pair)], pair_sem)[0]
    core = place[0] % 2
    rows = total.shape[0]
    half = rows // 2
    kv_groups = pair.shape[1] // (2 * HD)
    heads = q_all.shape[0] // rows
    count = heads // kv_groups
    local_heads = stats.shape[1] // 5
    chips = stats.shape[0] // 2
    for group in range(kv_groups):
        for head in range(group * count, (group + 1) * count):
            column = pl.multiple_of((core * heads + head) * HD, HD)
            for which, (own, sib, out) in enumerate(((q, q_sib, q_all), (g, g_sib, g_all))):
                for source, low in ((own, head * rows), (sib, head * rows + half)):
                    pltpu.make_async_copy(
                        source.at[:, pl.ds(column, HD)],
                        out.at[pl.ds(low, half), pl.ds(0, HD)],
                        sems.at[group, which],
                    ).start()

    def stat_rows(which, group):
        found = []
        for head in range(group * count, (group + 1) * count):
            source, local = divmod(head, local_heads)
            row = which * local_heads + local
            found.append(stats[core * chips + source, row : row + 1, :])
        return jnp.concatenate(found, axis=0)

    total[...] = jnp.zeros_like(total)
    lane = lax.broadcasted_iota(jnp.int32, (half, LANES), 1)
    level = lax.broadcasted_iota(jnp.int32, (LANES, HD), 0)
    level = jnp.where(level < K2, level, level - K2).astype(jnp.float32)
    for group in range(kv_groups):
        for out, base, sign in ((q_all, 0, -1.0 / FACTOR), (g_all, 2, -1.0)):
            for side in range(2):
                terms = split_terms(stat_rows(base + side, group) * sign, STAT_TERMS)
                terms = jnp.concatenate([term.astype(jnp.float32) for term in terms], axis=0)
                fill = jnp.zeros((LANES - terms.shape[0], half), jnp.float32)
                columns = jnp.concatenate([terms, fill], axis=0).T
                for head in range(count):
                    chosen = jnp.where(lane % count == head, columns, 0.0)
                    low = (group * count + head) * rows + side * half
                    out[low : low + half, HD:] = chosen.astype(jnp.bfloat16)
        codes = stat_rows(4, group)
        for head in range(count):
            code = codes[head : head + 1]
            sign = jnp.where(code >= K2, -1.0, 1.0)
            bucket = jnp.where(code >= K2, code - K2, code)
            table = jnp.where(level == bucket, sign, 0.0)
            low = (group * count + head) * HD
            tables[low : low + HD, :] = table.T.astype(jnp.bfloat16)
    pair_copy.wait()

    def own_block(group):
        key, value = (pair[:, at * HD : (at + 1) * HD] for at in (group, kv_groups + group))
        return jnp.concatenate([key, value], axis=1)

    for group in range(kv_groups):
        at = pl.ds(group * count * rows, count * rows)
        for which, out in enumerate((q_all, g_all)):
            side = out.at[at, pl.ds(0, HD)]
            pltpu.make_async_copy(side, side, sems.at[group, which]).wait()
        attend(
            place, start, q_all.at[at, :], g_all.at[at, :],
            tables.at[pl.ds(group * count * HD, count * HD), :],
            [own_block(group)], [0], True, total,
        )


def next_kernel(place, start, q_all, g_all, tables, before, *refs, steps, picked):
    blocks, total = refs[:-1], refs[-1]
    rows = total.shape[0]
    kv_groups = tables.shape[0] // HD // GROUP
    size = q_all.shape[0] // kv_groups
    width = tables.shape[0] // kv_groups
    chip = place[0] // 2

    def block_of(group):
        halves = [block for block in blocks if block.shape[1] == 2 * HD]
        wholes = [block for block in blocks if block.shape[1] != 2 * HD]
        found = [halves[picked.index(group)][...]] if halves else []
        if wholes:
            key, value = (
                wholes[0][:, at * HD : (at + 1) * HD] for at in (group, kv_groups + group)
            )
            found.append(jnp.concatenate([key, value], axis=1))
        return found[0] if len(found) == 1 else jnp.where(chip == max(steps), *found)

    step = jnp.int32(NO_STEP)
    for at_chip, known in steps.items():
        step = jnp.where(chip == at_chip, known, step)
    total[...] = before[...]

    @pl.when(step < NO_STEP)
    def _():
        for group in picked:
            at = pl.ds(group * size, size)
            attend(
                place, start, q_all.at[at, :], g_all.at[at, :],
                tables.at[pl.ds(group * width, width), :],
                [block_of(group)], [step], False, total,
            )


def last_kernel(
    place, start, q_all, g_all, tables, before, hi_own, hi_sib, *refs, steps, picked, scale
):
    blocks, out, total = refs[:-2], refs[-2], refs[-1]
    next_kernel(place, start, q_all, g_all, tables, before, *blocks, total, steps=steps, picked=picked)
    hashed = jnp.concatenate([hi_own[...], hi_sib[...]], axis=0)
    both = sum(dot_tn(hashed, part) for part in split_terms(total[...], 2))
    half = K1 // 2
    lane = lax.broadcasted_iota(jnp.int32, (half, LANES), 1)
    sketch = (jnp.where(lane < K2, both[:half], both[half:]) * scale).astype(out.dtype)
    parts, chunk = out.shape[1], out.shape[2]
    for part in range(parts):
        for doc in range(out.shape[0]):
            out[doc, part] = sketch[part * chunk : (part + 1) * chunk]


def score_kernel(place, recv_ref, stored_ref, own_ref, partial_ref, sums, flat, *, scale):
    docs, parts, chunk, _ = recv_ref.shape
    for doc in range(docs):
        sums[doc] = jnp.sum(recv_ref[doc].astype(jnp.float32), axis=0)
    for row in range(chunk):
        flat[:, row * LANES : (row + 1) * LANES] = sums[:, row, :]
        own_ref[:, row * LANES : (row + 1) * LANES] = sums[place[0], row : row + 1, :]
    pieces = split_terms(flat[...], 3)
    stacked = jnp.concatenate(pieces, axis=0)
    products = dot_nt(stacked, stored_ref[...])
    partial = (products[:docs] + products[docs : 2 * docs] + products[2 * docs :]) * scale
    if len(partial_ref.shape) == 3:
        for part in range(parts):
            partial_ref[part] = partial[:, part * LANES : (part + 1) * LANES]
    else:
        partial_ref[...] = partial


def local(
    queries,
    key_heads,
    value_heads,
    out_grad,
    log_sums,
    row_delta,
    doc_start,
    layer_input,
    hash_in,
    hash_out,
    query_sketch,
):
    ctx_count = lax.axis_size("ctx")
    docs = lax.axis_size("doc")
    chips = ctx_count // 2
    place = lax.axis_index("ctx").astype(jnp.int32).reshape(1)
    doc_place = lax.axis_index("doc").astype(jnp.int32).reshape(1)
    rows = queries.shape[1]
    seq_len = rows * ctx_count
    local_heads = log_sums.shape[1]
    core_heads = local_heads * chips
    kv_width = key_heads.shape[2]
    shape = jax.ShapeDtypeStruct
    params = lambda mib: pltpu.CompilerParams(vmem_limit_bytes=mib * MIB)

    def permute(array, target):
        pairs = [(i, target(i)) for i in range(ctx_count)]
        return lax.ppermute(array, "ctx", [pair for pair in pairs if pair[1] < ctx_count])

    swap = lambda array: permute(array, lambda i: i ^ 1)

    def pin(*arrays):
        return [pltpu.with_memory_space_constraint(array, pltpu.HBM) for array in arrays]

    def after(arrays, *done):
        return lax.optimization_barrier((tuple(arrays), done))[0]

    packed = pl.pallas_call(
        pack_kernel,
        out_shape=shape((ctx_count, 5 * local_heads, LANES), jnp.float32),
        in_specs=[ANY] * 3,
        out_specs=VMEM,
        scratch_shapes=[
            pltpu.VMEM((local_heads, seq_len), jnp.float32),
            pltpu.VMEM((local_heads, seq_len), jnp.float32),
            pltpu.VMEM((local_heads, HD), jnp.int32),
            pltpu.SemaphoreType.DMA((3,)),
        ],
        compiler_params=params(16),
    )(*pin(log_sums[0], row_delta[0], hash_out.reshape(local_heads, HD)))
    stats = lax.all_to_all(packed, "ctx", split_axis=0, concat_axis=0, tiled=True)

    q, g = queries[0], out_grad[0]
    q_sib, g_sib = (swap(array) for array in after((q, g), packed))

    half_shape = shape((rows, kv_width), jnp.bfloat16)
    pair_shape = shape((2 * rows, kv_width), jnp.bfloat16)
    pair, other = pl.pallas_call(
        prepare_kernel,
        out_shape=(pair_shape, half_shape),
        in_specs=[SMEM, ANY, ANY],
        out_specs=(ANY, VMEM),
        scratch_shapes=[pltpu.VMEM((rows, kv_width), jnp.bfloat16)] * 3
        + [pltpu.SemaphoreType.DMA((4,))],
        compiler_params=params(16),
    )(place, *pin(key_heads[0], value_heads[0]))
    from_sib = swap(other)

    groups = kv_width // (2 * HD)
    part_shape = shape((2 * rows, 2 * HD), jnp.bfloat16)
    pair, *halves = pl.pallas_call(
        join_kernel,
        out_shape=(pair_shape,) + (part_shape,) * groups,
        in_specs=[ANY, ANY, SMEM],
        out_specs=(ANY,) + (VMEM,) * groups,
        input_output_aliases={0: 0},
        scratch_shapes=[pltpu.SemaphoreType.DMA((1 + 4 * groups,))],
        compiler_params=params(16),
    )(*after((pair, from_sib), stats), doc_start)

    four = chips == 4
    if four:
        plan = [
            [(0, 2, 2), (2, 3, 1)],
            [(1, 3, 2), (0, 1, 1)],
            [(2, 3, 3), (1, 2, 1)],
        ]
    else:
        plan = [
            [(chip, chip + 1, wave + 1) for chip in range(wave, chips - 1)]
            for wave in range(chips - 1)
        ]

    def send(block, routes):
        route = {low: high for low, high, _ in routes}
        return permute(block, lambda i: 2 * route.get(i // 2, chips) + i % 2)

    received = [[send(half, plan[0]) for half in halves] if four else [send(pair, plan[0])]]
    if four:
        received.append([send(pair, plan[1])])

    stacked = shape((core_heads * 2 * rows, 2 * HD), jnp.bfloat16)
    table_shape = shape((core_heads * HD, LANES), jnp.bfloat16)
    total_shape = shape((2 * rows, LANES), jnp.float32)
    total, q_all, g_all, tables = pl.pallas_call(
        first_kernel,
        out_shape=(total_shape, stacked, stacked, table_shape),
        in_specs=[SMEM, SMEM, ANY, ANY, ANY, ANY, VMEM, ANY],
        out_specs=(VMEM, VMEM, VMEM, VMEM),
        scratch_shapes=[
            pltpu.VMEM((2 * rows, kv_width), jnp.bfloat16),
            pltpu.SemaphoreType.DMA((kv_width // (2 * HD), 2)),
            pltpu.SemaphoreType.DMA((1,)),
        ],
        compiler_params=params(24),
    )(place, doc_start, *pin(q), q_sib, *pin(g), g_sib, stats, pair)

    parts = max(1, layer_input.shape[2] // 1024)
    width = layer_input.shape[2] // parts
    hashed = pl.pallas_call(
        hash_kernel,
        out_shape=shape((rows, K1), jnp.bfloat16),
        in_specs=[ANY, ANY],
        out_specs=VMEM,
        scratch_shapes=[
            pltpu.VMEM((parts, rows, width), jnp.bfloat16),
            pltpu.VMEM((1, parts * width), jnp.int32),
            pltpu.SemaphoreType.DMA((1 + parts,)),
        ],
        compiler_params=params(16),
    )(*after((layer_input[0], hash_in.reshape(1, -1)), total))
    hashed_sib = swap(hashed)

    if four:
        passed = after(received[0], total)
        (own,) = after((pair,), total, received[0][0])
        received.append([send(half, plan[2][:1]) for half in passed])
        received[-1].append(send(own, plan[2][1:]))
    for wave in range(len(received), len(plan)):
        received.append([send(received[-1][0], plan[wave])])

    scale = (seq_len * layer_input.shape[2] // K1) ** -0.5
    chunk = K1 * K2 // LANES // ctx_count
    tiles = [
        (wave, range(groups), blocks) for wave, blocks in enumerate(received) if len(blocks) < 3
    ]
    if four:
        *halves, own = received[-1]
        tiles += [(2, [group], [half, own]) for group, half in enumerate(halves)]
    for wave, picked, blocks in tiles:
        last = blocks is tiles[-1][2]
        steps = {high: step for _, high, step in plan[wave]}
        given = dict(steps=steps, picked=list(picked))
        args = (place, doc_start, q_all, g_all, tables, total)
        if not last:
            total = pl.pallas_call(
                functools.partial(next_kernel, **given),
                out_shape=total_shape,
                in_specs=[SMEM, SMEM] + [VMEM] * (4 + len(blocks)),
                out_specs=VMEM,
                compiler_params=params(24),
            )(*args, *blocks)
            continue
        parts = pl.pallas_call(
            functools.partial(last_kernel, scale=scale, **given),
            out_shape=shape((docs, ctx_count, chunk, LANES), jnp.bfloat16),
            in_specs=[SMEM, SMEM] + [VMEM] * (6 + len(blocks)),
            out_specs=VMEM,
            scratch_shapes=[pltpu.VMEM((2 * rows, LANES), jnp.float32)],
            compiler_params=params(24),
        )(*args, hashed, hashed_sib, *blocks)

    parts = parts.reshape(-1, chunk, LANES)
    parts = lax.all_to_all(parts, ("doc", "ctx"), split_axis=0, concat_axis=0, tiled=True)
    parts = parts.reshape(docs, ctx_count, chunk, LANES)
    stored = query_sketch.shape[0]
    wide = stored // ctx_count == LANES
    partial_shape = (ctx_count, docs, LANES) if wide else (docs, stored)
    local_sketch, partial = pl.pallas_call(
        functools.partial(score_kernel, scale=(K1 * K2) ** -0.5),
        out_shape=(
            shape((1, chunk * LANES), jnp.float32),
            shape(partial_shape, jnp.float32),
        ),
        in_specs=[SMEM, VMEM, VMEM],
        out_specs=(VMEM, VMEM),
        scratch_shapes=[
            pltpu.VMEM((docs, chunk, LANES), jnp.float32),
            pltpu.VMEM((docs, chunk * LANES), jnp.float32),
        ],
        compiler_params=params(16),
    )(doc_place, parts, query_sketch)
    if not wide:
        partial = partial.reshape(docs, ctx_count, -1).transpose(1, 0, 2)
    partial = lax.all_to_all(partial, "ctx", split_axis=0, concat_axis=0, tiled=True)
    return local_sketch, jnp.sum(partial, axis=0)


def solution(mesh):
    return jax.shard_map(
        local,
        mesh=mesh,
        in_specs=(
            P("doc", "ctx", None),
            P("doc", "ctx", None),
            P("doc", "ctx", None),
            P("doc", "ctx", None),
            P("doc", "ctx", None),
            P("doc", "ctx", None),
            P("doc"),
            P("doc", "ctx", None),
            P(),
            P("ctx"),
            P("doc", "ctx"),
        ),
        out_specs=(P("doc", "ctx"), P(None, ("doc", "ctx"))),
        check_vma=False,
    )
```

```python
import functools

import jax
import jax.numpy as jnp
from jax import lax
from jax.experimental import pallas as pl
from jax.experimental.pallas import tpu as pltpu
from jax.sharding import PartitionSpec as P

HD = 128
K1 = 128
K2 = 64
LANES = 128
FACTOR = HD**-0.5
STAT_TERMS = 3
NO_STEP = 1024
GROUP = 8
MIB = 1024 * 1024
SMEM = pl.BlockSpec(memory_space=pltpu.SMEM)
VMEM = pl.BlockSpec(memory_space=pltpu.VMEM)
ANY = pl.BlockSpec(memory_space=pl.ANY)


def dot_nt(left, right):
    return lax.dot_general(
        left, right, (((1,), (1,)), ((), ())), preferred_element_type=jnp.float32
    )


def dot_tn(left, right):
    return lax.dot_general(
        left, right, (((0,), (0,)), ((), ())), preferred_element_type=jnp.float32
    )


def split_terms(value, terms):
    parts = []
    for _ in range(terms):
        part = value.astype(jnp.bfloat16)
        parts.append(part)
        value = value - part.astype(jnp.float32)
    return parts


def fetch(pairs, sems):
    copies = [
        pltpu.make_async_copy(source, target, sems.at[index])
        for index, (source, target) in enumerate(pairs)
    ]
    for copy in copies:
        copy.start()
    return copies


def pack_kernel(logs_in, deltas_in, codes_in, packed, logs, deltas, codes, sems):
    for copy in fetch(((logs_in, logs), (deltas_in, deltas), (codes_in, codes)), sems):
        copy.wait()
    heads = logs.shape[0]
    code_rows = codes[...].astype(jnp.float32)
    for target in range(packed.shape[0]):
        own = slice(target * LANES, (target + 1) * LANES)
        sib = slice((target ^ 1) * LANES, ((target ^ 1) + 1) * LANES)
        packed[target, :heads, :] = logs[:, own]
        packed[target, heads : 2 * heads, :] = logs[:, sib]
        packed[target, 2 * heads : 3 * heads, :] = deltas[:, own]
        packed[target, 3 * heads : 4 * heads, :] = deltas[:, sib]
        packed[target, 4 * heads :, :] = code_rows


def prepare_kernel(place, key_in, value_in, pair, other, key, value, mine, sems):
    rows = key.shape[0] // 2
    pieces = [pl.ds(low, rows) for low in (0, rows)]
    for copy in fetch(
        [
            (source.at[piece, :], target.at[piece, :])
            for piece in pieces
            for source, target in ((key_in, key), (value_in, value))
        ],
        sems,
    ):
        copy.wait()
    core = place[0] % 2
    half = key.shape[1] // 2
    for at_core in range(2):

        @pl.when(core == at_core)
        def _(at_core=at_core):
            near = slice(at_core * half, (at_core + 1) * half)
            far = slice((1 - at_core) * half, (2 - at_core) * half)
            mine[:, :half], mine[:, half:] = key[:, near], value[:, near]
            other[:, :half], other[:, half:] = key[:, far], value[:, far]

    for copy in fetch([(mine, pair.at[pl.ds(0, mine.shape[0]), :])], sems):
        copy.wait()


def join_kernel(_, lower, __, pair, *refs):
    parts, sems = refs[:-1], refs[-1]
    rows = lower.shape[0]
    copies = [(lower, pair.at[pl.ds(rows, rows), :])]
    for group, part in enumerate(parts):
        for half in range(2):
            at = pl.ds((half * len(parts) + group) * HD, HD)
            to = pl.ds(half * HD, HD)
            copies.append((pair.at[pl.ds(0, rows), at], part.at[pl.ds(0, rows), to]))
            copies.append((lower.at[:, at], part.at[pl.ds(rows, rows), to]))
    for copy in fetch(copies, sems):
        copy.wait()


def relay_kernel(place, own, received, out, sems, *, relaying):
    passing = place[0] // 2 == relaying

    @pl.when(passing)
    def _():
        fetch([(received, out)], sems)[0].wait()

    @pl.when(jnp.logical_not(passing))
    def _():
        fetch([(own, out)], sems)[0].wait()


def hash_kernel(rows_in, codes_in, out, rows, codes, sems):
    count, _, width = rows.shape
    pairs = [(codes_in, codes)]
    for part in range(count):
        pairs.append((rows_in.at[:, pl.ds(part * width, width)], rows.at[part]))
    copies = fetch(pairs, sems)
    copies[0].wait()
    level = lax.broadcasted_iota(jnp.int32, (K1, width), 0)
    level = jnp.where(level < K1 // 2, 2 * level, 2 * level - K1 + 1)
    total = jnp.zeros(out.shape, jnp.float32)
    for part in range(count):
        code = codes[:, part * width : (part + 1) * width]
        sign = jnp.where(code >= K1, -1.0, 1.0)
        bucket = jnp.where(code >= K1, code - K1, code)
        table = jnp.where(level == bucket, sign, 0.0).astype(jnp.bfloat16)
        copies[1 + part].wait()
        total += dot_nt(rows[part], table)
    out[...] = total.astype(out.dtype)


def attend(place, start, q_at, g_at, tables, blocks, steps, causal, total):
    core = place[0] % 2
    rows = total.shape[0]
    half = rows // 2
    count = q_at.shape[0] // rows
    own_base = place[0] * half
    sib_base = jnp.where(core == 0, own_base + half, own_base - half)
    index = lax.broadcasted_iota(jnp.int32, (rows, LANES), 0)
    spread = jnp.where(index < half, own_base + index, sib_base - half + index)
    lane = lax.broadcasted_iota(jnp.int32, (rows, LANES), 1)
    ones = jnp.where(lane < STAT_TERMS * count, 1.0, 0.0).astype(jnp.bfloat16)
    keys, key_sides, value_sides = [], [], []
    for block, step in zip(blocks, steps):
        seen = spread - step * rows >= start[0]
        keys.append(jnp.where(seen, block[:, :HD], jnp.zeros((), jnp.bfloat16)))
        key_sides.append(jnp.concatenate([keys[-1], ones], axis=1))
        value_sides.append(jnp.concatenate([block[:, HD:], ones], axis=1))
    if causal:
        shape = (rows, rows)
        row_at = lax.broadcasted_iota(jnp.int32, shape, 0)
        col_at = lax.broadcasted_iota(jnp.int32, shape, 1)
        row_at = jnp.where(row_at < half, own_base + row_at, sib_base - half + row_at)
        col_at = jnp.where(col_at < half, own_base + col_at, sib_base - half + col_at)
        visible = (col_at <= row_at)[None]
    parts = 2 if count % 2 == 0 else 1
    size = count * rows // parts
    hashed = []
    for part in range(parts):
        at = pl.ds(part * size, size)
        grads = None
        for key, key_side, value_side in zip(keys, key_sides, value_sides):
            logits = dot_nt(q_at[at, :], key_side) * FACTOR
            weights = jnp.exp(jnp.minimum(logits, 1.0))
            if causal and key is keys[0]:
                weights = weights.reshape(count // parts, rows, rows)
                weights = jnp.where(visible, weights, 0.0).reshape(size, rows)
            scores = (weights * dot_nt(g_at[at, :], value_side)).astype(jnp.bfloat16)
            product = jnp.dot(scores, key, preferred_element_type=jnp.float32)
            grads = product if grads is None else grads + product
        grads = (grads * FACTOR).astype(jnp.bfloat16)
        hashed += [grads[low : low + rows] for low in range(0, size, rows)]
    hashed = jnp.concatenate(hashed, axis=1)
    total[...] += jnp.dot(hashed, tables[...], preferred_element_type=jnp.float32)


def first_kernel(place, start, q, q_sib, g, g_sib, stats, pair_in, *refs):
    total, q_all, g_all, tables, pair, sems, pair_sem = refs
    pair_copy = fetch([(pair_in, pair)], pair_sem)[0]
    core = place[0] % 2
    rows = total.shape[0]
    half = rows // 2
    kv_groups = pair.shape[1] // (2 * HD)
    heads = q_all.shape[0] // rows
    count = heads // kv_groups
    local_heads = stats.shape[1] // 5
    chips = stats.shape[0] // 2
    for group in range(kv_groups):
        for head in range(group * count, (group + 1) * count):
            column = pl.multiple_of((core * heads + head) * HD, HD)
            for which, (own, sib, out) in enumerate(((q, q_sib, q_all), (g, g_sib, g_all))):
                for source, low in ((own, head * rows), (sib, head * rows + half)):
                    pltpu.make_async_copy(
                        source.at[:, pl.ds(column, HD)],
                        out.at[pl.ds(low, half), pl.ds(0, HD)],
                        sems.at[group, which],
                    ).start()

    def stat_rows(which, group):
        found = []
        for head in range(group * count, (group + 1) * count):
            source, local = divmod(head, local_heads)
            row = which * local_heads + local
            found.append(stats[core * chips + source, row : row + 1, :])
        return jnp.concatenate(found, axis=0)

    total[...] = jnp.zeros_like(total)
    lane = lax.broadcasted_iota(jnp.int32, (half, LANES), 1)
    level = lax.broadcasted_iota(jnp.int32, (LANES, HD), 0)
    level = jnp.where(level < K2, level, level - K2).astype(jnp.float32)
    for group in range(kv_groups):
        for out, base, sign in ((q_all, 0, -1.0 / FACTOR), (g_all, 2, -1.0)):
            for side in range(2):
                terms = split_terms(stat_rows(base + side, group) * sign, STAT_TERMS)
                terms = jnp.concatenate([term.astype(jnp.float32) for term in terms], axis=0)
                fill = jnp.zeros((LANES - terms.shape[0], half), jnp.float32)
                columns = jnp.concatenate([terms, fill], axis=0).T
                for head in range(count):
                    chosen = jnp.where(lane % count == head, columns, 0.0)
                    low = (group * count + head) * rows + side * half
                    out[low : low + half, HD:] = chosen.astype(jnp.bfloat16)
        codes = stat_rows(4, group)
        for head in range(count):
            code = codes[head : head + 1]
            sign = jnp.where(code >= K2, -1.0, 1.0)
            bucket = jnp.where(code >= K2, code - K2, code)
            table = jnp.where(level == bucket, sign, 0.0)
            low = (group * count + head) * HD
            tables[low : low + HD, :] = table.T.astype(jnp.bfloat16)
    pair_copy.wait()

    def own_block(group):
        key, value = (pair[:, at * HD : (at + 1) * HD] for at in (group, kv_groups + group))
        return jnp.concatenate([key, value], axis=1)

    for group in range(kv_groups):
        at = pl.ds(group * count * rows, count * rows)
        for which, out in enumerate((q_all, g_all)):
            side = out.at[at, pl.ds(0, HD)]
            pltpu.make_async_copy(side, side, sems.at[group, which]).wait()
        attend(
            place, start, q_all.at[at, :], g_all.at[at, :],
            tables.at[pl.ds(group * count * HD, count * HD), :],
            [own_block(group)], [0], True, total,
        )


def next_kernel(place, start, q_all, g_all, tables, before, *refs, steps, picked):
    blocks, total = refs[:-1], refs[-1]
    rows = total.shape[0]
    kv_groups = tables.shape[0] // HD // GROUP
    size = q_all.shape[0] // kv_groups
    width = tables.shape[0] // kv_groups
    chip = place[0] // 2

    def block_of(group):
        block = blocks[picked.index(group) % len(blocks)]
        if block.shape[1] == 2 * HD:
            return block[...]
        key, value = (block[:, at * HD : (at + 1) * HD] for at in (group, kv_groups + group))
        return jnp.concatenate([key, value], axis=1)

    step = jnp.int32(NO_STEP)
    for at_chip, known in steps.items():
        step = jnp.where(chip == at_chip, known, step)
    total[...] = before[...]

    @pl.when(step < NO_STEP)
    def _():
        for group in picked:
            at = pl.ds(group * size, size)
            attend(
                place, start, q_all.at[at, :], g_all.at[at, :],
                tables.at[pl.ds(group * width, width), :],
                [block_of(group)], [step], False, total,
            )


def last_kernel(
    place, start, q_all, g_all, tables, before, hi_own, hi_sib, *refs, steps, picked, scale
):
    blocks, out, total = refs[:-2], refs[-2], refs[-1]
    next_kernel(place, start, q_all, g_all, tables, before, *blocks, total, steps=steps, picked=picked)
    hashed = jnp.concatenate([hi_own[...], hi_sib[...]], axis=0)
    both = sum(dot_tn(hashed, part) for part in split_terms(total[...], 2))
    half = K1 // 2
    lane = lax.broadcasted_iota(jnp.int32, (half, LANES), 1)
    sketch = (jnp.where(lane < K2, both[:half], both[half:]) * scale).astype(out.dtype)
    parts, chunk = out.shape[1], out.shape[2]
    for part in range(parts):
        for doc in range(out.shape[0]):
            out[doc, part] = sketch[part * chunk : (part + 1) * chunk]


def score_kernel(place, recv_ref, stored_ref, own_ref, partial_ref, sums, flat, *, scale):
    docs, parts, chunk, _ = recv_ref.shape
    for doc in range(docs):
        sums[doc] = jnp.sum(recv_ref[doc].astype(jnp.float32), axis=0)
    for row in range(chunk):
        flat[:, row * LANES : (row + 1) * LANES] = sums[:, row, :]
        own_ref[:, row * LANES : (row + 1) * LANES] = sums[place[0], row : row + 1, :]
    pieces = split_terms(flat[...], 3)
    stacked = jnp.concatenate(pieces, axis=0)
    products = dot_nt(stacked, stored_ref[...])
    partial = (products[:docs] + products[docs : 2 * docs] + products[2 * docs :]) * scale
    if len(partial_ref.shape) == 3:
        for part in range(parts):
            partial_ref[part] = partial[:, part * LANES : (part + 1) * LANES]
    else:
        partial_ref[...] = partial


def local(
    queries,
    key_heads,
    value_heads,
    out_grad,
    log_sums,
    row_delta,
    doc_start,
    layer_input,
    hash_in,
    hash_out,
    query_sketch,
):
    ctx_count = lax.axis_size("ctx")
    docs = lax.axis_size("doc")
    chips = ctx_count // 2
    place = lax.axis_index("ctx").astype(jnp.int32).reshape(1)
    doc_place = lax.axis_index("doc").astype(jnp.int32).reshape(1)
    rows = queries.shape[1]
    seq_len = rows * ctx_count
    local_heads = log_sums.shape[1]
    core_heads = local_heads * chips
    kv_width = key_heads.shape[2]
    shape = jax.ShapeDtypeStruct
    params = lambda mib: pltpu.CompilerParams(vmem_limit_bytes=mib * MIB)

    def permute(array, target):
        pairs = [(i, target(i)) for i in range(ctx_count)]
        return lax.ppermute(array, "ctx", [pair for pair in pairs if pair[1] < ctx_count])

    swap = lambda array: permute(array, lambda i: i ^ 1)

    def pin(*arrays):
        return [pltpu.with_memory_space_constraint(array, pltpu.HBM) for array in arrays]

    def after(arrays, *done):
        return lax.optimization_barrier((tuple(arrays), done))[0]

    packed = pl.pallas_call(
        pack_kernel,
        out_shape=shape((ctx_count, 5 * local_heads, LANES), jnp.float32),
        in_specs=[ANY] * 3,
        out_specs=VMEM,
        scratch_shapes=[
            pltpu.VMEM((local_heads, seq_len), jnp.float32),
            pltpu.VMEM((local_heads, seq_len), jnp.float32),
            pltpu.VMEM((local_heads, HD), jnp.int32),
            pltpu.SemaphoreType.DMA((3,)),
        ],
        compiler_params=params(16),
    )(*pin(log_sums[0], row_delta[0], hash_out.reshape(local_heads, HD)))
    stats = lax.all_to_all(packed, "ctx", split_axis=0, concat_axis=0, tiled=True)

    q, g = queries[0], out_grad[0]
    q_sib, g_sib = (swap(array) for array in after((q, g), packed))

    half_shape = shape((rows, kv_width), jnp.bfloat16)
    pair_shape = shape((2 * rows, kv_width), jnp.bfloat16)
    pair, other = pl.pallas_call(
        prepare_kernel,
        out_shape=(pair_shape, half_shape),
        in_specs=[SMEM, ANY, ANY],
        out_specs=(ANY, VMEM),
        scratch_shapes=[pltpu.VMEM((rows, kv_width), jnp.bfloat16)] * 3
        + [pltpu.SemaphoreType.DMA((4,))],
        compiler_params=params(16),
    )(place, *pin(key_heads[0], value_heads[0]))
    from_sib = swap(other)

    groups = kv_width // (2 * HD)
    part_shape = shape((2 * rows, 2 * HD), jnp.bfloat16)
    pair, *halves = pl.pallas_call(
        join_kernel,
        out_shape=(pair_shape,) + (part_shape,) * groups,
        in_specs=[ANY, ANY, SMEM],
        out_specs=(ANY,) + (VMEM,) * groups,
        input_output_aliases={0: 0},
        scratch_shapes=[pltpu.SemaphoreType.DMA((1 + 4 * groups,))],
        compiler_params=params(16),
    )(*after((pair, from_sib), stats), doc_start)

    four = chips == 4
    if four:
        plan = [
            [(0, 2, 2), (2, 3, 1)],
            [(1, 3, 2), (0, 1, 1)],
            [(2, 3, 3), (1, 2, 1)],
        ]
    else:
        plan = [
            [(chip, chip + 1, wave + 1) for chip in range(wave, chips - 1)]
            for wave in range(chips - 1)
        ]

    def send(block, routes):
        route = {low: high for low, high, _ in routes}
        return permute(block, lambda i: 2 * route.get(i // 2, chips) + i % 2)

    received = [[send(half, plan[0]) for half in halves] if four else [send(pair, plan[0])]]
    if four:
        received.append([send(pair, plan[1])])

    stacked = shape((core_heads * 2 * rows, 2 * HD), jnp.bfloat16)
    table_shape = shape((core_heads * HD, LANES), jnp.bfloat16)
    total_shape = shape((2 * rows, LANES), jnp.float32)
    total, q_all, g_all, tables = pl.pallas_call(
        first_kernel,
        out_shape=(total_shape, stacked, stacked, table_shape),
        in_specs=[SMEM, SMEM, ANY, ANY, ANY, ANY, VMEM, ANY],
        out_specs=(VMEM, VMEM, VMEM, VMEM),
        scratch_shapes=[
            pltpu.VMEM((2 * rows, kv_width), jnp.bfloat16),
            pltpu.SemaphoreType.DMA((kv_width // (2 * HD), 2)),
            pltpu.SemaphoreType.DMA((1,)),
        ],
        compiler_params=params(24),
    )(place, doc_start, *pin(q), q_sib, *pin(g), g_sib, stats, pair)

    parts = max(1, layer_input.shape[2] // 1024)
    width = layer_input.shape[2] // parts
    hashed = pl.pallas_call(
        hash_kernel,
        out_shape=shape((rows, K1), jnp.bfloat16),
        in_specs=[ANY, ANY],
        out_specs=VMEM,
        scratch_shapes=[
            pltpu.VMEM((parts, rows, width), jnp.bfloat16),
            pltpu.VMEM((1, parts * width), jnp.int32),
            pltpu.SemaphoreType.DMA((1 + parts,)),
        ],
        compiler_params=params(16),
    )(*after((layer_input[0], hash_in.reshape(1, -1)), total))
    hashed_sib = swap(hashed)

    if four:
        relayed = []
        passed = list(after(received[0][:1], total))
        passed += after(received[0][1:], hashed)
        for own, block in zip(halves, passed):
            relayed.append(
                pl.pallas_call(
                    functools.partial(relay_kernel, relaying=2),
                    out_shape=part_shape,
                    in_specs=[SMEM, ANY, ANY],
                    out_specs=VMEM,
                    scratch_shapes=[pltpu.SemaphoreType.DMA((1,))],
                    compiler_params=params(16),
                )(place, own, block)
            )
        received.append([send(half, plan[2]) for half in relayed])
    for wave in range(len(received), len(plan)):
        received.append([send(received[-1][0], plan[wave])])

    scale = (seq_len * layer_input.shape[2] // K1) ** -0.5
    chunk = K1 * K2 // LANES // ctx_count
    tiles = [(wave, range(groups), blocks) for wave, blocks in enumerate(received)]
    if four:
        tiles[-1:] = [(2, [group], [half]) for group, half in enumerate(received[-1])]
    for wave, picked, blocks in tiles:
        last = blocks is tiles[-1][2]
        steps = {high: step for _, high, step in plan[wave]}
        given = dict(steps=steps, picked=list(picked))
        args = (place, doc_start, q_all, g_all, tables, total)
        if not last:
            total = pl.pallas_call(
                functools.partial(next_kernel, **given),
                out_shape=total_shape,
                in_specs=[SMEM, SMEM] + [VMEM] * (4 + len(blocks)),
                out_specs=VMEM,
                compiler_params=params(24),
            )(*args, *blocks)
            continue
        parts = pl.pallas_call(
            functools.partial(last_kernel, scale=scale, **given),
            out_shape=shape((docs, ctx_count, chunk, LANES), jnp.bfloat16),
            in_specs=[SMEM, SMEM] + [VMEM] * (6 + len(blocks)),
            out_specs=VMEM,
            scratch_shapes=[pltpu.VMEM((2 * rows, LANES), jnp.float32)],
            compiler_params=params(24),
        )(*args, hashed, hashed_sib, *blocks)

    parts = parts.reshape(-1, chunk, LANES)
    parts = lax.all_to_all(parts, ("doc", "ctx"), split_axis=0, concat_axis=0, tiled=True)
    parts = parts.reshape(docs, ctx_count, chunk, LANES)
    stored = query_sketch.shape[0]
    wide = stored // ctx_count == LANES
    partial_shape = (ctx_count, docs, LANES) if wide else (docs, stored)
    local_sketch, partial = pl.pallas_call(
        functools.partial(score_kernel, scale=(K1 * K2) ** -0.5),
        out_shape=(
            shape((1, chunk * LANES), jnp.float32),
            shape(partial_shape, jnp.float32),
        ),
        in_specs=[SMEM, VMEM, VMEM],
        out_specs=(VMEM, VMEM),
        scratch_shapes=[
            pltpu.VMEM((docs, chunk, LANES), jnp.float32),
            pltpu.VMEM((docs, chunk * LANES), jnp.float32),
        ],
        compiler_params=params(16),
    )(doc_place, parts, query_sketch)
    if not wide:
        partial = partial.reshape(docs, ctx_count, -1).transpose(1, 0, 2)
    partial = lax.all_to_all(partial, "ctx", split_axis=0, concat_axis=0, tiled=True)
    return local_sketch, jnp.sum(partial, axis=0)


def solution(mesh):
    return jax.shard_map(
        local,
        mesh=mesh,
        in_specs=(
            P("doc", "ctx", None),
            P("doc", "ctx", None),
            P("doc", "ctx", None),
            P("doc", "ctx", None),
            P("doc", "ctx", None),
            P("doc", "ctx", None),
            P("doc"),
            P("doc", "ctx", None),
            P(),
            P("ctx"),
            P("doc", "ctx"),
        ),
        out_specs=(P("doc", "ctx"), P(None, ("doc", "ctx"))),
        check_vma=False,
    )
```

```python
import functools

import jax
import jax.numpy as jnp
from jax import lax
from jax.experimental import pallas as pl
from jax.experimental.pallas import tpu as pltpu
from jax.sharding import PartitionSpec as P

HD = 128
K1 = 128
K2 = 64
LANES = 128
FACTOR = HD**-0.5
STAT_TERMS = 3
NO_STEP = 1024
GROUP = 8
MIB = 1024 * 1024
SMEM = pl.BlockSpec(memory_space=pltpu.SMEM)
VMEM = pl.BlockSpec(memory_space=pltpu.VMEM)
ANY = pl.BlockSpec(memory_space=pl.ANY)


def dot_nt(left, right):
    return lax.dot_general(
        left, right, (((1,), (1,)), ((), ())), preferred_element_type=jnp.float32
    )


def dot_tn(left, right):
    return lax.dot_general(
        left, right, (((0,), (0,)), ((), ())), preferred_element_type=jnp.float32
    )


def split_terms(value, terms):
    parts = []
    for _ in range(terms):
        part = value.astype(jnp.bfloat16)
        parts.append(part)
        value = value - part.astype(jnp.float32)
    return parts


def fetch(pairs, sems):
    copies = [
        pltpu.make_async_copy(source, target, sems.at[index])
        for index, (source, target) in enumerate(pairs)
    ]
    for copy in copies:
        copy.start()
    return copies


def pack_kernel(logs_in, deltas_in, codes_in, packed, logs, deltas, codes, sems):
    for copy in fetch(((logs_in, logs), (deltas_in, deltas), (codes_in, codes)), sems):
        copy.wait()
    heads = logs.shape[0]
    code_rows = codes[...].astype(jnp.float32)
    for target in range(packed.shape[0]):
        own = slice(target * LANES, (target + 1) * LANES)
        sib = slice((target ^ 1) * LANES, ((target ^ 1) + 1) * LANES)
        packed[target, :heads, :] = logs[:, own]
        packed[target, heads : 2 * heads, :] = logs[:, sib]
        packed[target, 2 * heads : 3 * heads, :] = deltas[:, own]
        packed[target, 3 * heads : 4 * heads, :] = deltas[:, sib]
        packed[target, 4 * heads :, :] = code_rows


def prepare_kernel(place, key_in, value_in, pair, other, key, value, mine, sems):
    rows = key.shape[0] // 2
    pieces = [pl.ds(low, rows) for low in (0, rows)]
    for copy in fetch(
        [
            (source.at[piece, :], target.at[piece, :])
            for piece in pieces
            for source, target in ((key_in, key), (value_in, value))
        ],
        sems,
    ):
        copy.wait()
    core = place[0] % 2
    half = key.shape[1] // 2
    for at_core in range(2):

        @pl.when(core == at_core)
        def _(at_core=at_core):
            near = slice(at_core * half, (at_core + 1) * half)
            far = slice((1 - at_core) * half, (2 - at_core) * half)
            mine[:, :half], mine[:, half:] = key[:, near], value[:, near]
            other[:, :half], other[:, half:] = key[:, far], value[:, far]

    for copy in fetch([(mine, pair.at[pl.ds(0, mine.shape[0]), :])], sems):
        copy.wait()


def join_kernel(_, lower, __, pair, sems):
    rows = lower.shape[0]
    for copy in fetch([(lower, pair.at[pl.ds(rows, rows), :])], sems):
        copy.wait()


def relay_kernel(place, own, received, *refs, relaying):
    parts, sems = refs[:-1], refs[-1]
    passing = place[0] // 2 == relaying

    def cut(block):
        copies = []
        for group, part in enumerate(parts):
            for half in range(2):
                at = pl.ds((half * len(parts) + group) * HD, HD)
                copies.append((block.at[:, at], part.at[:, pl.ds(half * HD, HD)]))
        for copy in fetch(copies, sems):
            copy.wait()

    @pl.when(passing)
    def _():
        cut(received)

    @pl.when(jnp.logical_not(passing))
    def _():
        cut(own)


def hash_kernel(rows_in, codes_in, out, rows, codes, sems):
    count, _, width = rows.shape
    pairs = [(codes_in, codes)]
    for part in range(count):
        pairs.append((rows_in.at[:, pl.ds(part * width, width)], rows.at[part]))
    copies = fetch(pairs, sems)
    copies[0].wait()
    level = lax.broadcasted_iota(jnp.int32, (K1, width), 0)
    level = jnp.where(level < K1 // 2, 2 * level, 2 * level - K1 + 1)
    total = jnp.zeros(out.shape, jnp.float32)
    for part in range(count):
        code = codes[:, part * width : (part + 1) * width]
        sign = jnp.where(code >= K1, -1.0, 1.0)
        bucket = jnp.where(code >= K1, code - K1, code)
        table = jnp.where(level == bucket, sign, 0.0).astype(jnp.bfloat16)
        copies[1 + part].wait()
        total += dot_nt(rows[part], table)
    out[...] = total.astype(out.dtype)


def attend(place, start, q_at, g_at, tables, blocks, steps, causal, total):
    core = place[0] % 2
    rows = total.shape[0]
    half = rows // 2
    count = q_at.shape[0] // rows
    own_base = place[0] * half
    sib_base = jnp.where(core == 0, own_base + half, own_base - half)
    index = lax.broadcasted_iota(jnp.int32, (rows, LANES), 0)
    spread = jnp.where(index < half, own_base + index, sib_base - half + index)
    lane = lax.broadcasted_iota(jnp.int32, (rows, LANES), 1)
    ones = jnp.where(lane < STAT_TERMS * count, 1.0, 0.0).astype(jnp.bfloat16)
    keys, key_sides, value_sides = [], [], []
    for block, step in zip(blocks, steps):
        seen = spread - step * rows >= start[0]
        keys.append(jnp.where(seen, block[:, :HD], jnp.zeros((), jnp.bfloat16)))
        key_sides.append(jnp.concatenate([keys[-1], ones], axis=1))
        value_sides.append(jnp.concatenate([block[:, HD:], ones], axis=1))
    if causal:
        shape = (rows, rows)
        row_at = lax.broadcasted_iota(jnp.int32, shape, 0)
        col_at = lax.broadcasted_iota(jnp.int32, shape, 1)
        row_at = jnp.where(row_at < half, own_base + row_at, sib_base - half + row_at)
        col_at = jnp.where(col_at < half, own_base + col_at, sib_base - half + col_at)
        visible = (col_at <= row_at)[None]
    parts = 2 if count % 2 == 0 else 1
    size = count * rows // parts
    hashed = []
    for part in range(parts):
        at = pl.ds(part * size, size)
        grads = None
        for key, key_side, value_side in zip(keys, key_sides, value_sides):
            logits = dot_nt(q_at[at, :], key_side) * FACTOR
            weights = jnp.exp(jnp.minimum(logits, 1.0))
            if causal and key is keys[0]:
                weights = weights.reshape(count // parts, rows, rows)
                weights = jnp.where(visible, weights, 0.0).reshape(size, rows)
            scores = (weights * dot_nt(g_at[at, :], value_side)).astype(jnp.bfloat16)
            product = jnp.dot(scores, key, preferred_element_type=jnp.float32)
            grads = product if grads is None else grads + product
        grads = (grads * FACTOR).astype(jnp.bfloat16)
        hashed += [grads[low : low + rows] for low in range(0, size, rows)]
    hashed = jnp.concatenate(hashed, axis=1)
    total[...] += jnp.dot(hashed, tables[...], preferred_element_type=jnp.float32)


def first_kernel(place, start, q, q_sib, g, g_sib, stats, pair_in, *refs):
    total, q_all, g_all, tables, pair, sems, pair_sem = refs
    pair_copy = fetch([(pair_in, pair)], pair_sem)[0]
    core = place[0] % 2
    rows = total.shape[0]
    half = rows // 2
    kv_groups = pair.shape[1] // (2 * HD)
    heads = q_all.shape[0] // rows
    count = heads // kv_groups
    local_heads = stats.shape[1] // 5
    chips = stats.shape[0] // 2
    for group in range(kv_groups):
        for head in range(group * count, (group + 1) * count):
            column = pl.multiple_of((core * heads + head) * HD, HD)
            for which, (own, sib, out) in enumerate(((q, q_sib, q_all), (g, g_sib, g_all))):
                for source, low in ((own, head * rows), (sib, head * rows + half)):
                    pltpu.make_async_copy(
                        source.at[:, pl.ds(column, HD)],
                        out.at[pl.ds(low, half), pl.ds(0, HD)],
                        sems.at[group, which],
                    ).start()

    def stat_rows(which, group):
        found = []
        for head in range(group * count, (group + 1) * count):
            source, local = divmod(head, local_heads)
            row = which * local_heads + local
            found.append(stats[core * chips + source, row : row + 1, :])
        return jnp.concatenate(found, axis=0)

    total[...] = jnp.zeros_like(total)
    lane = lax.broadcasted_iota(jnp.int32, (half, LANES), 1)
    level = lax.broadcasted_iota(jnp.int32, (LANES, HD), 0)
    level = jnp.where(level < K2, level, level - K2).astype(jnp.float32)
    for group in range(kv_groups):
        for out, base, sign in ((q_all, 0, -1.0 / FACTOR), (g_all, 2, -1.0)):
            for side in range(2):
                terms = split_terms(stat_rows(base + side, group) * sign, STAT_TERMS)
                terms = jnp.concatenate([term.astype(jnp.float32) for term in terms], axis=0)
                fill = jnp.zeros((LANES - terms.shape[0], half), jnp.float32)
                columns = jnp.concatenate([terms, fill], axis=0).T
                for head in range(count):
                    chosen = jnp.where(lane % count == head, columns, 0.0)
                    low = (group * count + head) * rows + side * half
                    out[low : low + half, HD:] = chosen.astype(jnp.bfloat16)
        codes = stat_rows(4, group)
        for head in range(count):
            code = codes[head : head + 1]
            sign = jnp.where(code >= K2, -1.0, 1.0)
            bucket = jnp.where(code >= K2, code - K2, code)
            table = jnp.where(level == bucket, sign, 0.0)
            low = (group * count + head) * HD
            tables[low : low + HD, :] = table.T.astype(jnp.bfloat16)
    pair_copy.wait()

    def own_block(group):
        key, value = (pair[:, at * HD : (at + 1) * HD] for at in (group, kv_groups + group))
        return jnp.concatenate([key, value], axis=1)

    for group in range(kv_groups):
        at = pl.ds(group * count * rows, count * rows)
        for which, out in enumerate((q_all, g_all)):
            side = out.at[at, pl.ds(0, HD)]
            pltpu.make_async_copy(side, side, sems.at[group, which]).wait()
        attend(
            place, start, q_all.at[at, :], g_all.at[at, :],
            tables.at[pl.ds(group * count * HD, count * HD), :],
            [own_block(group)], [0], True, total,
        )


def next_kernel(place, start, q_all, g_all, tables, before, *refs, steps, picked):
    blocks, total = refs[:-1], refs[-1]
    rows = total.shape[0]
    kv_groups = tables.shape[0] // HD // GROUP
    size = q_all.shape[0] // kv_groups
    width = tables.shape[0] // kv_groups
    chip = place[0] // 2

    def block_of(group):
        block = blocks[picked.index(group) % len(blocks)]
        if block.shape[1] == 2 * HD:
            return block[...]
        key, value = (block[:, at * HD : (at + 1) * HD] for at in (group, kv_groups + group))
        return jnp.concatenate([key, value], axis=1)

    step = jnp.int32(NO_STEP)
    for at_chip, known in steps.items():
        step = jnp.where(chip == at_chip, known, step)
    total[...] = before[...]

    @pl.when(step < NO_STEP)
    def _():
        for group in picked:
            at = pl.ds(group * size, size)
            attend(
                place, start, q_all.at[at, :], g_all.at[at, :],
                tables.at[pl.ds(group * width, width), :],
                [block_of(group)], [step], False, total,
            )


def last_kernel(
    place, start, q_all, g_all, tables, before, hi_own, hi_sib, *refs, steps, picked, scale
):
    blocks, out, total = refs[:-2], refs[-2], refs[-1]
    next_kernel(place, start, q_all, g_all, tables, before, *blocks, total, steps=steps, picked=picked)
    hashed = jnp.concatenate([hi_own[...], hi_sib[...]], axis=0)
    both = sum(dot_tn(hashed, part) for part in split_terms(total[...], 2))
    half = K1 // 2
    lane = lax.broadcasted_iota(jnp.int32, (half, LANES), 1)
    sketch = (jnp.where(lane < K2, both[:half], both[half:]) * scale).astype(out.dtype)
    parts, chunk = out.shape[1], out.shape[2]
    for part in range(parts):
        for doc in range(out.shape[0]):
            out[doc, part] = sketch[part * chunk : (part + 1) * chunk]


def score_kernel(place, recv_ref, stored_ref, own_ref, partial_ref, sums, flat, *, scale):
    docs, parts, chunk, _ = recv_ref.shape
    for doc in range(docs):
        sums[doc] = jnp.sum(recv_ref[doc].astype(jnp.float32), axis=0)
    for row in range(chunk):
        flat[:, row * LANES : (row + 1) * LANES] = sums[:, row, :]
        own_ref[:, row * LANES : (row + 1) * LANES] = sums[place[0], row : row + 1, :]
    pieces = split_terms(flat[...], 3)
    stacked = jnp.concatenate(pieces, axis=0)
    products = dot_nt(stacked, stored_ref[...])
    partial = (products[:docs] + products[docs : 2 * docs] + products[2 * docs :]) * scale
    if len(partial_ref.shape) == 3:
        for part in range(parts):
            partial_ref[part] = partial[:, part * LANES : (part + 1) * LANES]
    else:
        partial_ref[...] = partial


def local(
    queries,
    key_heads,
    value_heads,
    out_grad,
    log_sums,
    row_delta,
    doc_start,
    layer_input,
    hash_in,
    hash_out,
    query_sketch,
):
    ctx_count = lax.axis_size("ctx")
    docs = lax.axis_size("doc")
    chips = ctx_count // 2
    place = lax.axis_index("ctx").astype(jnp.int32).reshape(1)
    doc_place = lax.axis_index("doc").astype(jnp.int32).reshape(1)
    rows = queries.shape[1]
    seq_len = rows * ctx_count
    local_heads = log_sums.shape[1]
    core_heads = local_heads * chips
    kv_width = key_heads.shape[2]
    shape = jax.ShapeDtypeStruct
    params = lambda mib: pltpu.CompilerParams(vmem_limit_bytes=mib * MIB)

    def permute(array, target):
        pairs = [(i, target(i)) for i in range(ctx_count)]
        return lax.ppermute(array, "ctx", [pair for pair in pairs if pair[1] < ctx_count])

    swap = lambda array: permute(array, lambda i: i ^ 1)

    def pin(*arrays):
        return [pltpu.with_memory_space_constraint(array, pltpu.HBM) for array in arrays]

    def after(arrays, *done):
        return lax.optimization_barrier((tuple(arrays), done))[0]

    packed = pl.pallas_call(
        pack_kernel,
        out_shape=shape((ctx_count, 5 * local_heads, LANES), jnp.float32),
        in_specs=[ANY] * 3,
        out_specs=VMEM,
        scratch_shapes=[
            pltpu.VMEM((local_heads, seq_len), jnp.float32),
            pltpu.VMEM((local_heads, seq_len), jnp.float32),
            pltpu.VMEM((local_heads, HD), jnp.int32),
            pltpu.SemaphoreType.DMA((3,)),
        ],
        compiler_params=params(16),
    )(*pin(log_sums[0], row_delta[0], hash_out.reshape(local_heads, HD)))
    stats = lax.all_to_all(packed, "ctx", split_axis=0, concat_axis=0, tiled=True)

    q, g = queries[0], out_grad[0]
    q_sib, g_sib = (swap(array) for array in after((q, g), packed))

    half_shape = shape((rows, kv_width), jnp.bfloat16)
    pair_shape = shape((2 * rows, kv_width), jnp.bfloat16)
    pair, other = pl.pallas_call(
        prepare_kernel,
        out_shape=(pair_shape, half_shape),
        in_specs=[SMEM, ANY, ANY],
        out_specs=(ANY, VMEM),
        scratch_shapes=[pltpu.VMEM((rows, kv_width), jnp.bfloat16)] * 3
        + [pltpu.SemaphoreType.DMA((4,))],
        compiler_params=params(16),
    )(place, *pin(key_heads[0], value_heads[0]))
    from_sib = swap(other)

    groups = kv_width // (2 * HD)
    part_shape = shape((2 * rows, 2 * HD), jnp.bfloat16)
    pair = pl.pallas_call(
        join_kernel,
        out_shape=pair_shape,
        in_specs=[ANY, ANY, SMEM],
        out_specs=ANY,
        input_output_aliases={0: 0},
        scratch_shapes=[pltpu.SemaphoreType.DMA((1,))],
        compiler_params=params(16),
    )(*after((pair, from_sib), stats), doc_start)

    four = chips == 4
    if four:
        plan = [
            [(0, 2, 2), (2, 3, 1)],
            [(1, 3, 2), (0, 1, 1)],
            [(2, 3, 3), (1, 2, 1)],
        ]
    else:
        plan = [
            [(chip, chip + 1, wave + 1) for chip in range(wave, chips - 1)]
            for wave in range(chips - 1)
        ]

    def send(block, routes):
        route = {low: high for low, high, _ in routes}
        return permute(block, lambda i: 2 * route.get(i // 2, chips) + i % 2)

    received = [[send(pair, plan[0])]]

    stacked = shape((core_heads * 2 * rows, 2 * HD), jnp.bfloat16)
    table_shape = shape((core_heads * HD, LANES), jnp.bfloat16)
    total_shape = shape((2 * rows, LANES), jnp.float32)
    total, q_all, g_all, tables = pl.pallas_call(
        first_kernel,
        out_shape=(total_shape, stacked, stacked, table_shape),
        in_specs=[SMEM, SMEM, ANY, ANY, ANY, ANY, VMEM, ANY],
        out_specs=(VMEM, VMEM, VMEM, VMEM),
        scratch_shapes=[
            pltpu.VMEM((2 * rows, kv_width), jnp.bfloat16),
            pltpu.SemaphoreType.DMA((kv_width // (2 * HD), 2)),
            pltpu.SemaphoreType.DMA((1,)),
        ],
        compiler_params=params(24),
    )(place, doc_start, *pin(q), q_sib, *pin(g), g_sib, stats, pair)

    parts = max(1, layer_input.shape[2] // 1024)
    width = layer_input.shape[2] // parts
    hashed = pl.pallas_call(
        hash_kernel,
        out_shape=shape((rows, K1), jnp.bfloat16),
        in_specs=[ANY, ANY],
        out_specs=VMEM,
        scratch_shapes=[
            pltpu.VMEM((parts, rows, width), jnp.bfloat16),
            pltpu.VMEM((1, parts * width), jnp.int32),
            pltpu.SemaphoreType.DMA((1 + parts,)),
        ],
        compiler_params=params(16),
    )(*after((layer_input[0], hash_in.reshape(1, -1)), total))
    hashed_sib = swap(hashed)

    if four:
        (own,) = after((pair,), total)
        received.append([send(own, plan[1])])
        relayed = []
        halves = pl.pallas_call(
            functools.partial(relay_kernel, relaying=2),
            out_shape=(part_shape,) * groups,
            in_specs=[SMEM, ANY, ANY],
            out_specs=(VMEM,) * groups,
            scratch_shapes=[pltpu.SemaphoreType.DMA((2 * groups,))],
            compiler_params=params(16),
        )(place, *after((pair, received[0][0]), total, hashed))
        received.append([send(half, plan[2]) for half in halves])
    for wave in range(len(received), len(plan)):
        received.append([send(received[-1][0], plan[wave])])

    scale = (seq_len * layer_input.shape[2] // K1) ** -0.5
    chunk = K1 * K2 // LANES // ctx_count
    tiles = [(wave, range(groups), blocks) for wave, blocks in enumerate(received)]
    if four:
        tiles[-1:] = [(2, [group], [half]) for group, half in enumerate(received[-1])]
    for wave, picked, blocks in tiles:
        last = blocks is tiles[-1][2]
        steps = {high: step for _, high, step in plan[wave]}
        given = dict(steps=steps, picked=list(picked))
        args = (place, doc_start, q_all, g_all, tables, total)
        if not last:
            total = pl.pallas_call(
                functools.partial(next_kernel, **given),
                out_shape=total_shape,
                in_specs=[SMEM, SMEM] + [VMEM] * (4 + len(blocks)),
                out_specs=VMEM,
                compiler_params=params(24),
            )(*args, *blocks)
            continue
        parts = pl.pallas_call(
            functools.partial(last_kernel, scale=scale, **given),
            out_shape=shape((docs, ctx_count, chunk, LANES), jnp.bfloat16),
            in_specs=[SMEM, SMEM] + [VMEM] * (6 + len(blocks)),
            out_specs=VMEM,
            scratch_shapes=[pltpu.VMEM((2 * rows, LANES), jnp.float32)],
            compiler_params=params(24),
        )(*args, hashed, hashed_sib, *blocks)

    parts = parts.reshape(-1, chunk, LANES)
    parts = lax.all_to_all(parts, ("doc", "ctx"), split_axis=0, concat_axis=0, tiled=True)
    parts = parts.reshape(docs, ctx_count, chunk, LANES)
    stored = query_sketch.shape[0]
    wide = stored // ctx_count == LANES
    partial_shape = (ctx_count, docs, LANES) if wide else (docs, stored)
    local_sketch, partial = pl.pallas_call(
        functools.partial(score_kernel, scale=(K1 * K2) ** -0.5),
        out_shape=(
            shape((1, chunk * LANES), jnp.float32),
            shape(partial_shape, jnp.float32),
        ),
        in_specs=[SMEM, VMEM, VMEM],
        out_specs=(VMEM, VMEM),
        scratch_shapes=[
            pltpu.VMEM((docs, chunk, LANES), jnp.float32),
            pltpu.VMEM((docs, chunk * LANES), jnp.float32),
        ],
        compiler_params=params(16),
    )(doc_place, parts, query_sketch)
    if not wide:
        partial = partial.reshape(docs, ctx_count, -1).transpose(1, 0, 2)
    partial = lax.all_to_all(partial, "ctx", split_axis=0, concat_axis=0, tiled=True)
    return local_sketch, jnp.sum(partial, axis=0)


def solution(mesh):
    return jax.shard_map(
        local,
        mesh=mesh,
        in_specs=(
            P("doc", "ctx", None),
            P("doc", "ctx", None),
            P("doc", "ctx", None),
            P("doc", "ctx", None),
            P("doc", "ctx", None),
            P("doc", "ctx", None),
            P("doc"),
            P("doc", "ctx", None),
            P(),
            P("ctx"),
            P("doc", "ctx"),
        ),
        out_specs=(P("doc", "ctx"), P(None, ("doc", "ctx"))),
        check_vma=False,
    )
```

```python
import functools

import jax
import jax.numpy as jnp
from jax import lax
from jax.experimental import pallas as pl
from jax.experimental.pallas import tpu as pltpu
from jax.sharding import PartitionSpec as P

HD = 128
K1 = 128
K2 = 64
LANES = 128
FACTOR = HD**-0.5
STAT_TERMS = 3
NO_STEP = 1024
GROUP = 8
MIB = 1024 * 1024
SMEM = pl.BlockSpec(memory_space=pltpu.SMEM)
VMEM = pl.BlockSpec(memory_space=pltpu.VMEM)
ANY = pl.BlockSpec(memory_space=pl.ANY)


def dot_nt(left, right):
    return lax.dot_general(
        left, right, (((1,), (1,)), ((), ())), preferred_element_type=jnp.float32
    )


def dot_tn(left, right):
    return lax.dot_general(
        left, right, (((0,), (0,)), ((), ())), preferred_element_type=jnp.float32
    )


def split_terms(value, terms):
    parts = []
    for _ in range(terms):
        part = value.astype(jnp.bfloat16)
        parts.append(part)
        value = value - part.astype(jnp.float32)
    return parts


def fetch(pairs, sems):
    copies = [
        pltpu.make_async_copy(source, target, sems.at[index])
        for index, (source, target) in enumerate(pairs)
    ]
    for copy in copies:
        copy.start()
    return copies


def pack_kernel(logs_in, deltas_in, codes_in, packed, logs, deltas, codes, sems):
    for copy in fetch(((logs_in, logs), (deltas_in, deltas), (codes_in, codes)), sems):
        copy.wait()
    heads = logs.shape[0]
    code_rows = codes[...].astype(jnp.float32)
    for target in range(packed.shape[0]):
        own = slice(target * LANES, (target + 1) * LANES)
        sib = slice((target ^ 1) * LANES, ((target ^ 1) + 1) * LANES)
        packed[target, :heads, :] = logs[:, own]
        packed[target, heads : 2 * heads, :] = logs[:, sib]
        packed[target, 2 * heads : 3 * heads, :] = deltas[:, own]
        packed[target, 3 * heads : 4 * heads, :] = deltas[:, sib]
        packed[target, 4 * heads :, :] = code_rows


def prepare_kernel(place, key_in, value_in, pair, other, key, value, mine, sems):
    rows = key.shape[0] // 2
    pieces = [pl.ds(low, rows) for low in (0, rows)]
    for copy in fetch(
        [
            (source.at[piece, :], target.at[piece, :])
            for piece in pieces
            for source, target in ((key_in, key), (value_in, value))
        ],
        sems,
    ):
        copy.wait()
    core = place[0] % 2
    half = key.shape[1] // 2
    for at_core in range(2):

        @pl.when(core == at_core)
        def _(at_core=at_core):
            near = slice(at_core * half, (at_core + 1) * half)
            far = slice((1 - at_core) * half, (2 - at_core) * half)
            mine[:, :half], mine[:, half:] = key[:, near], value[:, near]
            other[:, :half], other[:, half:] = key[:, far], value[:, far]

    for copy in fetch([(mine, pair.at[pl.ds(0, mine.shape[0]), :])], sems):
        copy.wait()


def join_kernel(_, lower, __, pair, sems):
    rows = lower.shape[0]
    for copy in fetch([(lower, pair.at[pl.ds(rows, rows), :])], sems):
        copy.wait()


def relay_kernel(place, own, received, *refs, relaying):
    parts, sems = refs[:-1], refs[-1]
    passing = place[0] // 2 == relaying

    def cut(block):
        copies = []
        for group, part in enumerate(parts):
            for half in range(2):
                at = pl.ds((half * len(parts) + group) * HD, HD)
                copies.append((block.at[:, at], part.at[:, pl.ds(half * HD, HD)]))
        for copy in fetch(copies, sems):
            copy.wait()

    @pl.when(passing)
    def _():
        cut(received)

    @pl.when(jnp.logical_not(passing))
    def _():
        cut(own)


def hash_kernel(rows_in, codes_in, out, rows, codes, sems):
    count, _, width = rows.shape
    pairs = [(codes_in, codes)]
    for part in range(count):
        pairs.append((rows_in.at[:, pl.ds(part * width, width)], rows.at[part]))
    copies = fetch(pairs, sems)
    copies[0].wait()
    level = lax.broadcasted_iota(jnp.int32, (K1, width), 0)
    level = jnp.where(level < K1 // 2, 2 * level, 2 * level - K1 + 1)
    total = jnp.zeros(out.shape, jnp.float32)
    for part in range(count):
        code = codes[:, part * width : (part + 1) * width]
        sign = jnp.where(code >= K1, -1.0, 1.0)
        bucket = jnp.where(code >= K1, code - K1, code)
        table = jnp.where(level == bucket, sign, 0.0).astype(jnp.bfloat16)
        copies[1 + part].wait()
        total += dot_nt(rows[part], table)
    out[...] = total.astype(out.dtype)


def attend(place, start, q_at, g_at, tables, blocks, steps, causal, total):
    core = place[0] % 2
    rows = total.shape[0]
    half = rows // 2
    count = q_at.shape[0] // rows
    own_base = place[0] * half
    sib_base = jnp.where(core == 0, own_base + half, own_base - half)
    index = lax.broadcasted_iota(jnp.int32, (rows, LANES), 0)
    spread = jnp.where(index < half, own_base + index, sib_base - half + index)
    lane = lax.broadcasted_iota(jnp.int32, (rows, LANES), 1)
    ones = jnp.where(lane < STAT_TERMS * count, 1.0, 0.0).astype(jnp.bfloat16)
    keys, key_sides, value_sides = [], [], []
    for block, step in zip(blocks, steps):
        seen = spread - step * rows >= start[0]
        keys.append(jnp.where(seen, block[:, :HD], jnp.zeros((), jnp.bfloat16)))
        key_sides.append(jnp.concatenate([keys[-1], ones], axis=1))
        value_sides.append(jnp.concatenate([block[:, HD:], ones], axis=1))
    if causal:
        shape = (rows, rows)
        row_at = lax.broadcasted_iota(jnp.int32, shape, 0)
        col_at = lax.broadcasted_iota(jnp.int32, shape, 1)
        row_at = jnp.where(row_at < half, own_base + row_at, sib_base - half + row_at)
        col_at = jnp.where(col_at < half, own_base + col_at, sib_base - half + col_at)
        visible = (col_at <= row_at)[None]
    parts = 2 if count % 2 == 0 else 1
    size = count * rows // parts
    hashed = []
    for part in range(parts):
        at = pl.ds(part * size, size)
        grads = None
        for key, key_side, value_side in zip(keys, key_sides, value_sides):
            logits = dot_nt(q_at[at, :], key_side) * FACTOR
            weights = jnp.exp(jnp.minimum(logits, 1.0))
            if causal and key is keys[0]:
                weights = weights.reshape(count // parts, rows, rows)
                weights = jnp.where(visible, weights, 0.0).reshape(size, rows)
            scores = (weights * dot_nt(g_at[at, :], value_side)).astype(jnp.bfloat16)
            product = jnp.dot(scores, key, preferred_element_type=jnp.float32)
            grads = product if grads is None else grads + product
        grads = (grads * FACTOR).astype(jnp.bfloat16)
        hashed += [grads[low : low + rows] for low in range(0, size, rows)]
    hashed = jnp.concatenate(hashed, axis=1)
    total[...] += jnp.dot(hashed, tables[...], preferred_element_type=jnp.float32)


def first_kernel(place, start, q, q_sib, g, g_sib, stats, pair_in, *refs):
    total, q_all, g_all, tables, pair, sems, pair_sem = refs
    pair_copy = fetch([(pair_in, pair)], pair_sem)[0]
    core = place[0] % 2
    rows = total.shape[0]
    half = rows // 2
    kv_groups = pair.shape[1] // (2 * HD)
    heads = q_all.shape[0] // rows
    count = heads // kv_groups
    local_heads = stats.shape[1] // 5
    chips = stats.shape[0] // 2
    for group in range(kv_groups):
        for head in range(group * count, (group + 1) * count):
            column = pl.multiple_of((core * heads + head) * HD, HD)
            for which, (own, sib, out) in enumerate(((q, q_sib, q_all), (g, g_sib, g_all))):
                for source, low in ((own, head * rows), (sib, head * rows + half)):
                    pltpu.make_async_copy(
                        source.at[:, pl.ds(column, HD)],
                        out.at[pl.ds(low, half), pl.ds(0, HD)],
                        sems.at[group, which],
                    ).start()

    def stat_rows(which, group):
        found = []
        for head in range(group * count, (group + 1) * count):
            source, local = divmod(head, local_heads)
            row = which * local_heads + local
            found.append(stats[core * chips + source, row : row + 1, :])
        return jnp.concatenate(found, axis=0)

    total[...] = jnp.zeros_like(total)
    lane = lax.broadcasted_iota(jnp.int32, (half, LANES), 1)
    level = lax.broadcasted_iota(jnp.int32, (LANES, HD), 0)
    level = jnp.where(level < K2, level, level - K2).astype(jnp.float32)
    for group in range(kv_groups):
        for out, base, sign in ((q_all, 0, -1.0 / FACTOR), (g_all, 2, -1.0)):
            for side in range(2):
                terms = split_terms(stat_rows(base + side, group) * sign, STAT_TERMS)
                terms = jnp.concatenate([term.astype(jnp.float32) for term in terms], axis=0)
                fill = jnp.zeros((LANES - terms.shape[0], half), jnp.float32)
                columns = jnp.concatenate([terms, fill], axis=0).T
                for head in range(count):
                    chosen = jnp.where(lane % count == head, columns, 0.0)
                    low = (group * count + head) * rows + side * half
                    out[low : low + half, HD:] = chosen.astype(jnp.bfloat16)
        codes = stat_rows(4, group)
        for head in range(count):
            code = codes[head : head + 1]
            sign = jnp.where(code >= K2, -1.0, 1.0)
            bucket = jnp.where(code >= K2, code - K2, code)
            table = jnp.where(level == bucket, sign, 0.0)
            low = (group * count + head) * HD
            tables[low : low + HD, :] = table.T.astype(jnp.bfloat16)
    pair_copy.wait()

    def own_block(group):
        key, value = (pair[:, at * HD : (at + 1) * HD] for at in (group, kv_groups + group))
        return jnp.concatenate([key, value], axis=1)

    for group in range(kv_groups):
        at = pl.ds(group * count * rows, count * rows)
        for which, out in enumerate((q_all, g_all)):
            side = out.at[at, pl.ds(0, HD)]
            pltpu.make_async_copy(side, side, sems.at[group, which]).wait()
        attend(
            place, start, q_all.at[at, :], g_all.at[at, :],
            tables.at[pl.ds(group * count * HD, count * HD), :],
            [own_block(group)], [0], True, total,
        )


def next_kernel(place, start, q_all, g_all, tables, before, *refs, steps, picked):
    blocks, total = refs[:-1], refs[-1]
    rows = total.shape[0]
    kv_groups = tables.shape[0] // HD // GROUP
    size = q_all.shape[0] // kv_groups
    width = tables.shape[0] // kv_groups
    chip = place[0] // 2

    def block_of(group):
        block = blocks[picked.index(group) % len(blocks)]
        if block.shape[1] == 2 * HD:
            return block[...]
        key, value = (block[:, at * HD : (at + 1) * HD] for at in (group, kv_groups + group))
        return jnp.concatenate([key, value], axis=1)

    step = jnp.int32(NO_STEP)
    for at_chip, known in steps.items():
        step = jnp.where(chip == at_chip, known, step)
    total[...] = before[...]

    @pl.when(step < NO_STEP)
    def _():
        for group in picked:
            at = pl.ds(group * size, size)
            attend(
                place, start, q_all.at[at, :], g_all.at[at, :],
                tables.at[pl.ds(group * width, width), :],
                [block_of(group)], [step], False, total,
            )


def last_kernel(
    place, start, q_all, g_all, tables, before, hi_own, hi_sib, *refs, steps, picked, scale
):
    blocks, out, total = refs[:-2], refs[-2], refs[-1]
    next_kernel(place, start, q_all, g_all, tables, before, *blocks, total, steps=steps, picked=picked)
    hashed = jnp.concatenate([hi_own[...], hi_sib[...]], axis=0)
    both = sum(dot_tn(hashed, part) for part in split_terms(total[...], 2))
    half = K1 // 2
    lane = lax.broadcasted_iota(jnp.int32, (half, LANES), 1)
    sketch = (jnp.where(lane < K2, both[:half], both[half:]) * scale).astype(out.dtype)
    parts, chunk = out.shape[1], out.shape[2]
    for part in range(parts):
        for doc in range(out.shape[0]):
            out[doc, part] = sketch[part * chunk : (part + 1) * chunk]


def score_kernel(place, recv_ref, stored_ref, own_ref, partial_ref, sums, flat, *, scale):
    docs, parts, chunk, _ = recv_ref.shape
    for doc in range(docs):
        sums[doc] = jnp.sum(recv_ref[doc].astype(jnp.float32), axis=0)
    for row in range(chunk):
        flat[:, row * LANES : (row + 1) * LANES] = sums[:, row, :]
        own_ref[:, row * LANES : (row + 1) * LANES] = sums[place[0], row : row + 1, :]
    pieces = split_terms(flat[...], 3)
    stacked = jnp.concatenate(pieces, axis=0)
    products = dot_nt(stacked, stored_ref[...])
    partial = (products[:docs] + products[docs : 2 * docs] + products[2 * docs :]) * scale
    if len(partial_ref.shape) == 3:
        for part in range(parts):
            partial_ref[part] = partial[:, part * LANES : (part + 1) * LANES]
    else:
        partial_ref[...] = partial


def local(
    queries,
    key_heads,
    value_heads,
    out_grad,
    log_sums,
    row_delta,
    doc_start,
    layer_input,
    hash_in,
    hash_out,
    query_sketch,
):
    ctx_count = lax.axis_size("ctx")
    docs = lax.axis_size("doc")
    chips = ctx_count // 2
    place = lax.axis_index("ctx").astype(jnp.int32).reshape(1)
    doc_place = lax.axis_index("doc").astype(jnp.int32).reshape(1)
    rows = queries.shape[1]
    seq_len = rows * ctx_count
    local_heads = log_sums.shape[1]
    core_heads = local_heads * chips
    kv_width = key_heads.shape[2]
    shape = jax.ShapeDtypeStruct
    params = lambda mib: pltpu.CompilerParams(vmem_limit_bytes=mib * MIB)

    def permute(array, target):
        pairs = [(i, target(i)) for i in range(ctx_count)]
        return lax.ppermute(array, "ctx", [pair for pair in pairs if pair[1] < ctx_count])

    swap = lambda array: permute(array, lambda i: i ^ 1)

    def pin(*arrays):
        return [pltpu.with_memory_space_constraint(array, pltpu.HBM) for array in arrays]

    def after(arrays, *done):
        return lax.optimization_barrier((tuple(arrays), done))[0]

    packed = pl.pallas_call(
        pack_kernel,
        out_shape=shape((ctx_count, 5 * local_heads, LANES), jnp.float32),
        in_specs=[ANY] * 3,
        out_specs=VMEM,
        scratch_shapes=[
            pltpu.VMEM((local_heads, seq_len), jnp.float32),
            pltpu.VMEM((local_heads, seq_len), jnp.float32),
            pltpu.VMEM((local_heads, HD), jnp.int32),
            pltpu.SemaphoreType.DMA((3,)),
        ],
        compiler_params=params(16),
    )(*pin(log_sums[0], row_delta[0], hash_out.reshape(local_heads, HD)))
    stats = lax.all_to_all(packed, "ctx", split_axis=0, concat_axis=0, tiled=True)

    q, g = queries[0], out_grad[0]
    q_sib, g_sib = (swap(array) for array in after((q, g), packed))

    half_shape = shape((rows, kv_width), jnp.bfloat16)
    pair_shape = shape((2 * rows, kv_width), jnp.bfloat16)
    pair, other = pl.pallas_call(
        prepare_kernel,
        out_shape=(pair_shape, half_shape),
        in_specs=[SMEM, ANY, ANY],
        out_specs=(ANY, VMEM),
        scratch_shapes=[pltpu.VMEM((rows, kv_width), jnp.bfloat16)] * 3
        + [pltpu.SemaphoreType.DMA((4,))],
        compiler_params=params(16),
    )(place, *pin(key_heads[0], value_heads[0]))
    from_sib = swap(other)

    groups = kv_width // (2 * HD)
    part_shape = shape((2 * rows, 2 * HD), jnp.bfloat16)
    pair = pl.pallas_call(
        join_kernel,
        out_shape=pair_shape,
        in_specs=[ANY, ANY, SMEM],
        out_specs=ANY,
        input_output_aliases={0: 0},
        scratch_shapes=[pltpu.SemaphoreType.DMA((1,))],
        compiler_params=params(16),
    )(*after((pair, from_sib), packed), doc_start)

    four = chips == 4
    if four:
        plan = [
            [(0, 2, 2), (2, 3, 1)],
            [(1, 3, 2), (0, 1, 1)],
            [(2, 3, 3), (1, 2, 1)],
        ]
    else:
        plan = [
            [(chip, chip + 1, wave + 1) for chip in range(wave, chips - 1)]
            for wave in range(chips - 1)
        ]

    def send(block, routes):
        route = {low: high for low, high, _ in routes}
        return permute(block, lambda i: 2 * route.get(i // 2, chips) + i % 2)

    received = [[send(pair, plan[0])]]

    stacked = shape((core_heads * 2 * rows, 2 * HD), jnp.bfloat16)
    table_shape = shape((core_heads * HD, LANES), jnp.bfloat16)
    total_shape = shape((2 * rows, LANES), jnp.float32)
    total, q_all, g_all, tables = pl.pallas_call(
        first_kernel,
        out_shape=(total_shape, stacked, stacked, table_shape),
        in_specs=[SMEM, SMEM, ANY, ANY, ANY, ANY, VMEM, ANY],
        out_specs=(VMEM, VMEM, VMEM, VMEM),
        scratch_shapes=[
            pltpu.VMEM((2 * rows, kv_width), jnp.bfloat16),
            pltpu.SemaphoreType.DMA((kv_width // (2 * HD), 2)),
            pltpu.SemaphoreType.DMA((1,)),
        ],
        compiler_params=params(24),
    )(place, doc_start, *pin(q), q_sib, *pin(g), g_sib, stats, pair)

    parts = max(1, layer_input.shape[2] // 1024)
    width = layer_input.shape[2] // parts
    hashed = pl.pallas_call(
        hash_kernel,
        out_shape=shape((rows, K1), jnp.bfloat16),
        in_specs=[ANY, ANY],
        out_specs=VMEM,
        scratch_shapes=[
            pltpu.VMEM((parts, rows, width), jnp.bfloat16),
            pltpu.VMEM((1, parts * width), jnp.int32),
            pltpu.SemaphoreType.DMA((1 + parts,)),
        ],
        compiler_params=params(16),
    )(*after((layer_input[0], hash_in.reshape(1, -1)), total))
    hashed_sib = swap(hashed)

    if four:
        (own,) = after((pair,), stats)
        received.append([send(own, plan[1])])
        relayed = []
        halves = pl.pallas_call(
            functools.partial(relay_kernel, relaying=2),
            out_shape=(part_shape,) * groups,
            in_specs=[SMEM, ANY, ANY],
            out_specs=(VMEM,) * groups,
            scratch_shapes=[pltpu.SemaphoreType.DMA((2 * groups,))],
            compiler_params=params(16),
        )(place, *after((pair, received[0][0]), total, hashed))
        received.append([send(half, plan[2]) for half in halves])
    for wave in range(len(received), len(plan)):
        received.append([send(received[-1][0], plan[wave])])

    scale = (seq_len * layer_input.shape[2] // K1) ** -0.5
    chunk = K1 * K2 // LANES // ctx_count
    tiles = [(wave, range(groups), blocks) for wave, blocks in enumerate(received)]
    if four:
        tiles[-1:] = [(2, [group], [half]) for group, half in enumerate(received[-1])]
    for wave, picked, blocks in tiles:
        last = blocks is tiles[-1][2]
        steps = {high: step for _, high, step in plan[wave]}
        given = dict(steps=steps, picked=list(picked))
        args = (place, doc_start, q_all, g_all, tables, total)
        if not last:
            total = pl.pallas_call(
                functools.partial(next_kernel, **given),
                out_shape=total_shape,
                in_specs=[SMEM, SMEM] + [VMEM] * (4 + len(blocks)),
                out_specs=VMEM,
                compiler_params=params(24),
            )(*args, *blocks)
            continue
        parts = pl.pallas_call(
            functools.partial(last_kernel, scale=scale, **given),
            out_shape=shape((docs, ctx_count, chunk, LANES), jnp.bfloat16),
            in_specs=[SMEM, SMEM] + [VMEM] * (6 + len(blocks)),
            out_specs=VMEM,
            scratch_shapes=[pltpu.VMEM((2 * rows, LANES), jnp.float32)],
            compiler_params=params(24),
        )(*args, hashed, hashed_sib, *blocks)

    parts = parts.reshape(-1, chunk, LANES)
    parts = lax.all_to_all(parts, ("doc", "ctx"), split_axis=0, concat_axis=0, tiled=True)
    parts = parts.reshape(docs, ctx_count, chunk, LANES)
    stored = query_sketch.shape[0]
    wide = stored // ctx_count == LANES
    partial_shape = (ctx_count, docs, LANES) if wide else (docs, stored)
    local_sketch, partial = pl.pallas_call(
        functools.partial(score_kernel, scale=(K1 * K2) ** -0.5),
        out_shape=(
            shape((1, chunk * LANES), jnp.float32),
            shape(partial_shape, jnp.float32),
        ),
        in_specs=[SMEM, VMEM, VMEM],
        out_specs=(VMEM, VMEM),
        scratch_shapes=[
            pltpu.VMEM((docs, chunk, LANES), jnp.float32),
            pltpu.VMEM((docs, chunk * LANES), jnp.float32),
        ],
        compiler_params=params(16),
    )(doc_place, parts, query_sketch)
    if not wide:
        partial = partial.reshape(docs, ctx_count, -1).transpose(1, 0, 2)
    partial = lax.all_to_all(partial, "ctx", split_axis=0, concat_axis=0, tiled=True)
    return local_sketch, jnp.sum(partial, axis=0)


def solution(mesh):
    return jax.shard_map(
        local,
        mesh=mesh,
        in_specs=(
            P("doc", "ctx", None),
            P("doc", "ctx", None),
            P("doc", "ctx", None),
            P("doc", "ctx", None),
            P("doc", "ctx", None),
            P("doc", "ctx", None),
            P("doc"),
            P("doc", "ctx", None),
            P(),
            P("ctx"),
            P("doc", "ctx"),
        ),
        out_specs=(P("doc", "ctx"), P(None, ("doc", "ctx"))),
        check_vma=False,
    )
```

```python
import functools

import jax
import jax.numpy as jnp
from jax import lax
from jax.experimental import pallas as pl
from jax.experimental.pallas import tpu as pltpu
from jax.sharding import PartitionSpec as P

HD = 128
K1 = 128
K2 = 64
LANES = 128
FACTOR = HD**-0.5
STAT_TERMS = 3
NO_STEP = 1024
GROUP = 8
MIB = 1024 * 1024
SMEM = pl.BlockSpec(memory_space=pltpu.SMEM)
VMEM = pl.BlockSpec(memory_space=pltpu.VMEM)
ANY = pl.BlockSpec(memory_space=pl.ANY)


def dot_nt(left, right):
    return lax.dot_general(
        left, right, (((1,), (1,)), ((), ())), preferred_element_type=jnp.float32
    )


def dot_tn(left, right):
    return lax.dot_general(
        left, right, (((0,), (0,)), ((), ())), preferred_element_type=jnp.float32
    )


def split_terms(value, terms):
    parts = []
    for _ in range(terms):
        part = value.astype(jnp.bfloat16)
        parts.append(part)
        value = value - part.astype(jnp.float32)
    return parts


def fetch(pairs, sems):
    copies = [
        pltpu.make_async_copy(source, target, sems.at[index])
        for index, (source, target) in enumerate(pairs)
    ]
    for copy in copies:
        copy.start()
    return copies


def first_step_kernel(place, logs_in, deltas_in, codes_in, key_in, value_in, packed, pair, other, logs, deltas, codes, key, value, mine, sems, more_sems):
    copies = fetch(((key_in, key), (value_in, value)), more_sems)
    pack_kernel(logs_in, deltas_in, codes_in, packed, logs, deltas, codes, sems)
    prepare_kernel(place, copies, pair, other, key, value, mine, sems)


def pack_kernel(logs_in, deltas_in, codes_in, packed, logs, deltas, codes, sems):
    for copy in fetch(((logs_in, logs), (deltas_in, deltas), (codes_in, codes)), sems):
        copy.wait()
    heads = logs.shape[0]
    code_rows = codes[...].astype(jnp.float32)
    for target in range(packed.shape[0]):
        own = slice(target * LANES, (target + 1) * LANES)
        sib = slice((target ^ 1) * LANES, ((target ^ 1) + 1) * LANES)
        packed[target, :heads, :] = logs[:, own]
        packed[target, heads : 2 * heads, :] = logs[:, sib]
        packed[target, 2 * heads : 3 * heads, :] = deltas[:, own]
        packed[target, 3 * heads : 4 * heads, :] = deltas[:, sib]
        packed[target, 4 * heads :, :] = code_rows


def prepare_kernel(place, copies, pair, other, key, value, mine, sems):
    for copy in copies:
        copy.wait()
    core = place[0] % 2
    half = key.shape[1] // 2
    for at_core in range(2):

        @pl.when(core == at_core)
        def _(at_core=at_core):
            near = slice(at_core * half, (at_core + 1) * half)
            far = slice((1 - at_core) * half, (2 - at_core) * half)
            mine[:, :half], mine[:, half:] = key[:, near], value[:, near]
            other[:, :half], other[:, half:] = key[:, far], value[:, far]

    for copy in fetch([(mine, pair.at[pl.ds(0, mine.shape[0]), :])], sems):
        copy.wait()


def join_kernel(_, lower, __, pair, sems):
    rows = lower.shape[0]
    for copy in fetch([(lower, pair.at[pl.ds(rows, rows), :])], sems):
        copy.wait()


def relay_kernel(place, own, received, *refs, relaying):
    parts, sems = refs[:-1], refs[-1]
    passing = place[0] // 2 == relaying

    def cut(block):
        copies = []
        for group, part in enumerate(parts):
            for half in range(2):
                at = pl.ds((half * len(parts) + group) * HD, HD)
                copies.append((block.at[:, at], part.at[:, pl.ds(half * HD, HD)]))
        for copy in fetch(copies, sems):
            copy.wait()

    @pl.when(passing)
    def _():
        cut(received)

    @pl.when(jnp.logical_not(passing))
    def _():
        cut(own)


def hash_kernel(rows_in, codes_in, out, rows, codes, sems):
    count, _, width = rows.shape
    pairs = [(codes_in, codes)]
    for part in range(count):
        pairs.append((rows_in.at[:, pl.ds(part * width, width)], rows.at[part]))
    copies = fetch(pairs, sems)
    copies[0].wait()
    level = lax.broadcasted_iota(jnp.int32, (K1, width), 0)
    level = jnp.where(level < K1 // 2, 2 * level, 2 * level - K1 + 1)
    total = jnp.zeros(out.shape, jnp.float32)
    for part in range(count):
        code = codes[:, part * width : (part + 1) * width]
        sign = jnp.where(code >= K1, -1.0, 1.0)
        bucket = jnp.where(code >= K1, code - K1, code)
        table = jnp.where(level == bucket, sign, 0.0).astype(jnp.bfloat16)
        copies[1 + part].wait()
        total += dot_nt(rows[part], table)
    out[...] = total.astype(out.dtype)


def attend(place, start, q_at, g_at, tables, blocks, steps, causal, total):
    core = place[0] % 2
    rows = total.shape[0]
    half = rows // 2
    count = q_at.shape[0] // rows
    own_base = place[0] * half
    sib_base = jnp.where(core == 0, own_base + half, own_base - half)
    index = lax.broadcasted_iota(jnp.int32, (rows, LANES), 0)
    spread = jnp.where(index < half, own_base + index, sib_base - half + index)
    lane = lax.broadcasted_iota(jnp.int32, (rows, LANES), 1)
    ones = jnp.where(lane < STAT_TERMS * count, 1.0, 0.0).astype(jnp.bfloat16)
    keys, key_sides, value_sides = [], [], []
    for block, step in zip(blocks, steps):
        seen = spread - step * rows >= start[0]
        keys.append(jnp.where(seen, block[:, :HD], jnp.zeros((), jnp.bfloat16)))
        key_sides.append(jnp.concatenate([keys[-1], ones], axis=1))
        value_sides.append(jnp.concatenate([block[:, HD:], ones], axis=1))
    if causal:
        shape = (rows, rows)
        row_at = lax.broadcasted_iota(jnp.int32, shape, 0)
        col_at = lax.broadcasted_iota(jnp.int32, shape, 1)
        row_at = jnp.where(row_at < half, own_base + row_at, sib_base - half + row_at)
        col_at = jnp.where(col_at < half, own_base + col_at, sib_base - half + col_at)
        visible = (col_at <= row_at)[None]
    parts = 2 if count % 2 == 0 else 1
    size = count * rows // parts
    hashed = []
    for part in range(parts):
        at = pl.ds(part * size, size)
        grads = None
        for key, key_side, value_side in zip(keys, key_sides, value_sides):
            logits = dot_nt(q_at[at, :], key_side) * FACTOR
            weights = jnp.exp(jnp.minimum(logits, 1.0))
            if causal and key is keys[0]:
                weights = weights.reshape(count // parts, rows, rows)
                weights = jnp.where(visible, weights, 0.0).reshape(size, rows)
            scores = (weights * dot_nt(g_at[at, :], value_side)).astype(jnp.bfloat16)
            product = jnp.dot(scores, key, preferred_element_type=jnp.float32)
            grads = product if grads is None else grads + product
        grads = (grads * FACTOR).astype(jnp.bfloat16)
        hashed += [grads[low : low + rows] for low in range(0, size, rows)]
    hashed = jnp.concatenate(hashed, axis=1)
    total[...] += jnp.dot(hashed, tables[...], preferred_element_type=jnp.float32)


def first_kernel(place, start, q, q_sib, g, g_sib, stats, pair_in, *refs):
    total, q_all, g_all, tables, pair, sems, pair_sem = refs
    pair_copy = fetch([(pair_in, pair)], pair_sem)[0]
    core = place[0] % 2
    rows = total.shape[0]
    half = rows // 2
    kv_groups = pair.shape[1] // (2 * HD)
    heads = q_all.shape[0] // rows
    count = heads // kv_groups
    local_heads = stats.shape[1] // 5
    chips = stats.shape[0] // 2
    for group in range(kv_groups):
        for head in range(group * count, (group + 1) * count):
            column = pl.multiple_of((core * heads + head) * HD, HD)
            for which, (own, sib, out) in enumerate(((q, q_sib, q_all), (g, g_sib, g_all))):
                for source, low in ((own, head * rows), (sib, head * rows + half)):
                    pltpu.make_async_copy(
                        source.at[:, pl.ds(column, HD)],
                        out.at[pl.ds(low, half), pl.ds(0, HD)],
                        sems.at[group, which],
                    ).start()

    def stat_rows(which, group):
        found = []
        for head in range(group * count, (group + 1) * count):
            source, local = divmod(head, local_heads)
            row = which * local_heads + local
            found.append(stats[core * chips + source, row : row + 1, :])
        return jnp.concatenate(found, axis=0)

    total[...] = jnp.zeros_like(total)
    lane = lax.broadcasted_iota(jnp.int32, (half, LANES), 1)
    level = lax.broadcasted_iota(jnp.int32, (LANES, HD), 0)
    level = jnp.where(level < K2, level, level - K2).astype(jnp.float32)
    for group in range(kv_groups):
        for out, base, sign in ((q_all, 0, -1.0 / FACTOR), (g_all, 2, -1.0)):
            for side in range(2):
                terms = split_terms(stat_rows(base + side, group) * sign, STAT_TERMS)
                terms = jnp.concatenate([term.astype(jnp.float32) for term in terms], axis=0)
                fill = jnp.zeros((LANES - terms.shape[0], half), jnp.float32)
                columns = jnp.concatenate([terms, fill], axis=0).T
                for head in range(count):
                    chosen = jnp.where(lane % count == head, columns, 0.0)
                    low = (group * count + head) * rows + side * half
                    out[low : low + half, HD:] = chosen.astype(jnp.bfloat16)
        codes = stat_rows(4, group)
        for head in range(count):
            code = codes[head : head + 1]
            sign = jnp.where(code >= K2, -1.0, 1.0)
            bucket = jnp.where(code >= K2, code - K2, code)
            table = jnp.where(level == bucket, sign, 0.0)
            low = (group * count + head) * HD
            tables[low : low + HD, :] = table.T.astype(jnp.bfloat16)
    pair_copy.wait()

    def own_block(group):
        key, value = (pair[:, at * HD : (at + 1) * HD] for at in (group, kv_groups + group))
        return jnp.concatenate([key, value], axis=1)

    for group in range(kv_groups):
        at = pl.ds(group * count * rows, count * rows)
        for which, out in enumerate((q_all, g_all)):
            side = out.at[at, pl.ds(0, HD)]
            pltpu.make_async_copy(side, side, sems.at[group, which]).wait()
        attend(
            place, start, q_all.at[at, :], g_all.at[at, :],
            tables.at[pl.ds(group * count * HD, count * HD), :],
            [own_block(group)], [0], True, total,
        )


def next_kernel(place, start, q_all, g_all, tables, before, *refs, steps, picked):
    blocks, total = refs[:-1], refs[-1]
    rows = total.shape[0]
    kv_groups = tables.shape[0] // HD // GROUP
    size = q_all.shape[0] // kv_groups
    width = tables.shape[0] // kv_groups
    chip = place[0] // 2

    def block_of(group):
        block = blocks[picked.index(group) % len(blocks)]
        if block.shape[1] == 2 * HD:
            return block[...]
        key, value = (block[:, at * HD : (at + 1) * HD] for at in (group, kv_groups + group))
        return jnp.concatenate([key, value], axis=1)

    step = jnp.int32(NO_STEP)
    for at_chip, known in steps.items():
        step = jnp.where(chip == at_chip, known, step)
    total[...] = before[...]

    @pl.when(step < NO_STEP)
    def _():
        for group in picked:
            at = pl.ds(group * size, size)
            attend(
                place, start, q_all.at[at, :], g_all.at[at, :],
                tables.at[pl.ds(group * width, width), :],
                [block_of(group)], [step], False, total,
            )


def last_kernel(
    place, start, q_all, g_all, tables, before, hi_own, hi_sib, *refs, steps, picked, scale
):
    blocks, out, total = refs[:-2], refs[-2], refs[-1]
    next_kernel(place, start, q_all, g_all, tables, before, *blocks, total, steps=steps, picked=picked)
    hashed = jnp.concatenate([hi_own[...], hi_sib[...]], axis=0)
    both = sum(dot_tn(hashed, part) for part in split_terms(total[...], 2))
    half = K1 // 2
    lane = lax.broadcasted_iota(jnp.int32, (half, LANES), 1)
    sketch = (jnp.where(lane < K2, both[:half], both[half:]) * scale).astype(out.dtype)
    parts, chunk = out.shape[1], out.shape[2]
    for part in range(parts):
        for doc in range(out.shape[0]):
            out[doc, part] = sketch[part * chunk : (part + 1) * chunk]


def score_kernel(place, recv_ref, stored_ref, own_ref, partial_ref, sums, flat, *, scale):
    docs, parts, chunk, _ = recv_ref.shape
    for doc in range(docs):
        sums[doc] = jnp.sum(recv_ref[doc].astype(jnp.float32), axis=0)
    for row in range(chunk):
        flat[:, row * LANES : (row + 1) * LANES] = sums[:, row, :]
        own_ref[:, row * LANES : (row + 1) * LANES] = sums[place[0], row : row + 1, :]
    pieces = split_terms(flat[...], 3)
    stacked = jnp.concatenate(pieces, axis=0)
    products = dot_nt(stacked, stored_ref[...])
    partial = (products[:docs] + products[docs : 2 * docs] + products[2 * docs :]) * scale
    if len(partial_ref.shape) == 3:
        for part in range(parts):
            partial_ref[part] = partial[:, part * LANES : (part + 1) * LANES]
    else:
        partial_ref[...] = partial


def local(
    queries,
    key_heads,
    value_heads,
    out_grad,
    log_sums,
    row_delta,
    doc_start,
    layer_input,
    hash_in,
    hash_out,
    query_sketch,
):
    ctx_count = lax.axis_size("ctx")
    docs = lax.axis_size("doc")
    chips = ctx_count // 2
    place = lax.axis_index("ctx").astype(jnp.int32).reshape(1)
    doc_place = lax.axis_index("doc").astype(jnp.int32).reshape(1)
    rows = queries.shape[1]
    seq_len = rows * ctx_count
    local_heads = log_sums.shape[1]
    core_heads = local_heads * chips
    kv_width = key_heads.shape[2]
    shape = jax.ShapeDtypeStruct
    params = lambda mib: pltpu.CompilerParams(vmem_limit_bytes=mib * MIB)

    def permute(array, target):
        pairs = [(i, target(i)) for i in range(ctx_count)]
        return lax.ppermute(array, "ctx", [pair for pair in pairs if pair[1] < ctx_count])

    swap = lambda array: permute(array, lambda i: i ^ 1)

    def pin(*arrays):
        return [pltpu.with_memory_space_constraint(array, pltpu.HBM) for array in arrays]

    def after(arrays, *done):
        return lax.optimization_barrier((tuple(arrays), done))[0]

    half_shape = shape((rows, kv_width), jnp.bfloat16)
    pair_shape = shape((2 * rows, kv_width), jnp.bfloat16)
    packed, pair, other = pl.pallas_call(
        first_step_kernel,
        out_shape=(
            shape((ctx_count, 5 * local_heads, LANES), jnp.float32), pair_shape, half_shape,
        ),
        in_specs=[SMEM] + [ANY] * 5,
        out_specs=(VMEM, ANY, VMEM),
        scratch_shapes=[
            pltpu.VMEM((local_heads, seq_len), jnp.float32),
            pltpu.VMEM((local_heads, seq_len), jnp.float32),
            pltpu.VMEM((local_heads, HD), jnp.int32),
        ]
        + [pltpu.VMEM((rows, kv_width), jnp.bfloat16)] * 3
        + [pltpu.SemaphoreType.DMA((3,)), pltpu.SemaphoreType.DMA((2,))],
        compiler_params=params(16),
    )(
        place,
        *pin(
            log_sums[0], row_delta[0], hash_out.reshape(local_heads, HD),
            key_heads[0], value_heads[0],
        ),
    )
    stats = lax.all_to_all(packed, "ctx", split_axis=0, concat_axis=0, tiled=True)

    q, g = queries[0], out_grad[0]
    q_sib, g_sib = (swap(array) for array in after((q, g), packed))

    from_sib = swap(other)

    groups = kv_width // (2 * HD)
    part_shape = shape((2 * rows, 2 * HD), jnp.bfloat16)
    pair = pl.pallas_call(
        join_kernel,
        out_shape=pair_shape,
        in_specs=[ANY, ANY, SMEM],
        out_specs=ANY,
        input_output_aliases={0: 0},
        scratch_shapes=[pltpu.SemaphoreType.DMA((1,))],
        compiler_params=params(16),
    )(*after((pair, from_sib), packed), doc_start)

    four = chips == 4
    if four:
        plan = [
            [(0, 2, 2), (2, 3, 1)],
            [(1, 3, 2), (0, 1, 1)],
            [(2, 3, 3), (1, 2, 1)],
        ]
    else:
        plan = [
            [(chip, chip + 1, wave + 1) for chip in range(wave, chips - 1)]
            for wave in range(chips - 1)
        ]

    def send(block, routes):
        route = {low: high for low, high, _ in routes}
        return permute(block, lambda i: 2 * route.get(i // 2, chips) + i % 2)

    received = [[send(pair, plan[0])]]

    stacked = shape((core_heads * 2 * rows, 2 * HD), jnp.bfloat16)
    table_shape = shape((core_heads * HD, LANES), jnp.bfloat16)
    total_shape = shape((2 * rows, LANES), jnp.float32)
    total, q_all, g_all, tables = pl.pallas_call(
        first_kernel,
        out_shape=(total_shape, stacked, stacked, table_shape),
        in_specs=[SMEM, SMEM, ANY, ANY, ANY, ANY, VMEM, ANY],
        out_specs=(VMEM, VMEM, VMEM, VMEM),
        scratch_shapes=[
            pltpu.VMEM((2 * rows, kv_width), jnp.bfloat16),
            pltpu.SemaphoreType.DMA((kv_width // (2 * HD), 2)),
            pltpu.SemaphoreType.DMA((1,)),
        ],
        compiler_params=params(24),
    )(place, doc_start, *pin(q), q_sib, *pin(g), g_sib, stats, pair)

    parts = max(1, layer_input.shape[2] // 1024)
    width = layer_input.shape[2] // parts
    hashed = pl.pallas_call(
        hash_kernel,
        out_shape=shape((rows, K1), jnp.bfloat16),
        in_specs=[ANY, ANY],
        out_specs=VMEM,
        scratch_shapes=[
            pltpu.VMEM((parts, rows, width), jnp.bfloat16),
            pltpu.VMEM((1, parts * width), jnp.int32),
            pltpu.SemaphoreType.DMA((1 + parts,)),
        ],
        compiler_params=params(16),
    )(*after((layer_input[0], hash_in.reshape(1, -1)), total))
    hashed_sib = swap(hashed)

    if four:
        (own,) = after((pair,), stats)
        received.append([send(own, plan[1])])
        relayed = []
        halves = pl.pallas_call(
            functools.partial(relay_kernel, relaying=2),
            out_shape=(part_shape,) * groups,
            in_specs=[SMEM, ANY, ANY],
            out_specs=(VMEM,) * groups,
            scratch_shapes=[pltpu.SemaphoreType.DMA((2 * groups,))],
            compiler_params=params(16),
        )(place, *after((pair, received[0][0]), total, hashed))
        received.append([send(half, plan[2]) for half in halves])
    for wave in range(len(received), len(plan)):
        received.append([send(received[-1][0], plan[wave])])

    scale = (seq_len * layer_input.shape[2] // K1) ** -0.5
    chunk = K1 * K2 // LANES // ctx_count
    tiles = [(wave, range(groups), blocks) for wave, blocks in enumerate(received)]
    if four:
        tiles[-1:] = [(2, [group], [half]) for group, half in enumerate(received[-1])]
    for wave, picked, blocks in tiles:
        last = blocks is tiles[-1][2]
        steps = {high: step for _, high, step in plan[wave]}
        given = dict(steps=steps, picked=list(picked))
        args = (place, doc_start, q_all, g_all, tables, total)
        if not last:
            total = pl.pallas_call(
                functools.partial(next_kernel, **given),
                out_shape=total_shape,
                in_specs=[SMEM, SMEM] + [VMEM] * (4 + len(blocks)),
                out_specs=VMEM,
                compiler_params=params(24),
            )(*args, *blocks)
            continue
        parts = pl.pallas_call(
            functools.partial(last_kernel, scale=scale, **given),
            out_shape=shape((docs, ctx_count, chunk, LANES), jnp.bfloat16),
            in_specs=[SMEM, SMEM] + [VMEM] * (6 + len(blocks)),
            out_specs=VMEM,
            scratch_shapes=[pltpu.VMEM((2 * rows, LANES), jnp.float32)],
            compiler_params=params(24),
        )(*args, hashed, hashed_sib, *blocks)

    parts = parts.reshape(-1, chunk, LANES)
    parts = lax.all_to_all(parts, ("doc", "ctx"), split_axis=0, concat_axis=0, tiled=True)
    parts = parts.reshape(docs, ctx_count, chunk, LANES)
    stored = query_sketch.shape[0]
    wide = stored // ctx_count == LANES
    partial_shape = (ctx_count, docs, LANES) if wide else (docs, stored)
    local_sketch, partial = pl.pallas_call(
        functools.partial(score_kernel, scale=(K1 * K2) ** -0.5),
        out_shape=(
            shape((1, chunk * LANES), jnp.float32),
            shape(partial_shape, jnp.float32),
        ),
        in_specs=[SMEM, VMEM, VMEM],
        out_specs=(VMEM, VMEM),
        scratch_shapes=[
            pltpu.VMEM((docs, chunk, LANES), jnp.float32),
            pltpu.VMEM((docs, chunk * LANES), jnp.float32),
        ],
        compiler_params=params(16),
    )(doc_place, parts, query_sketch)
    if not wide:
        partial = partial.reshape(docs, ctx_count, -1).transpose(1, 0, 2)
    partial = lax.all_to_all(partial, "ctx", split_axis=0, concat_axis=0, tiled=True)
    return local_sketch, jnp.sum(partial, axis=0)


def solution(mesh):
    return jax.shard_map(
        local,
        mesh=mesh,
        in_specs=(
            P("doc", "ctx", None),
            P("doc", "ctx", None),
            P("doc", "ctx", None),
            P("doc", "ctx", None),
            P("doc", "ctx", None),
            P("doc", "ctx", None),
            P("doc"),
            P("doc", "ctx", None),
            P(),
            P("ctx"),
            P("doc", "ctx"),
        ),
        out_specs=(P("doc", "ctx"), P(None, ("doc", "ctx"))),
        check_vma=False,
    )
```
